256 devices in a mesh: section: 2 (over x_lo), dp: 16 (over z, core), tensor: 8 (over y, x_hi).
Axes of the slice: x: 4 (x_hi: 2, x_lo: 2; x = x_hi * 2 + x_lo), y: 4, z: 8, core: 2. Of those that a mesh axis runs over, the one named last changes fastest.
Arguments:
- cache_keys: bfloat16 [2, 256, 512, 1024], P(None, ('section', 'dp'), None, 'tensor'), may hold values from -5 to 5
- cache_values: bfloat16 [2, 256, 512, 1024], P(None, ('section', 'dp'), None, 'tensor'), may hold values from -5 to 5
- span_ids: int32 [32, 8], P('dp'), may hold values from 0 to 255, as said below
- owner_slot: int32 [256], replicated, may hold values from 0 to 255, as said below
- recompute_rows: int32 [256, 76], replicated, may hold values from 0 to 511, as said below
- hidden: bfloat16 [2, 32, 8, 76, 8192], P('section', 'dp', None, None, 'tensor'), may hold values from -6 to 6
- w_key: bfloat16 [2, 8192, 1024], P('section', 'tensor'), may hold values from -0.0625 to 0.0625
- w_value: bfloat16 [2, 8192, 1024], P('section', 'tensor'), may hold values from -0.0625 to 0.0625
- queries: bfloat16 [2, 32, 256, 8192], P('section', 'dp', None, 'tensor')
- query_keys: bfloat16 [2, 32, 256, 1024], P('section', 'dp', None, 'tensor')
- query_values: bfloat16 [2, 32, 256, 1024], P('section', 'dp', None, 'tensor'), may hold values from -5 to 5
Outputs:
- attended: bfloat16 [2, 32, 256, 8192], P('section', 'dp', None, 'tensor')
The draws below stay inside these ranges and needn't reach their ends.
Inputs may be any that keep to these rules, and one draw needn't show every extreme that they name: `owner_slot`: A permutation: each storage row holds one span; the owner of storage row s is the device s // 8 of section+dp. `span_ids`: the 16 spans named by the requests of one dp index lie on as many different owners. `recompute_rows`: each span's 76 rows are different.
All inputs are finite; a program needn't handle non-finite values.
Results may differ from the reference program's by a relative error of at most 0.02.
Values may be sent and summed in bfloat16 or wider, within the bound.
No kernel may reach another device: no remote copies, remote signals or barrier semaphores. Data moves between devices by JAX's collectives and lax.ppermute only.
A program may use at most 128 MiB of HBM per device.

```python
import jax
import jax.numpy as jnp
from jax import lax

D = 8192
QH = 64
KVH = 8
HD = 128
TOPK = 8
CLEN = 512
RROWS = 76
QLEN = 256
REQ_DEV = 2
CH_DEV = 8
LAYERS = 2
REQS = 32
SPANS = 256
N_TENSOR = 8


def retrieval_layout(key):
    perm_key, pop_key, score_key, row_key = jax.random.split(key, 4)
    slot_of = jax.random.permutation(perm_key, SPANS).astype(jnp.int32)
    span_at = jnp.argsort(slot_of, stable=True).astype(jnp.int32)
    owners = SPANS // CH_DEV
    blocks = REQS // REQ_DEV
    entries = REQ_DEV * TOPK
    weight = 1 + jax.random.randint(pop_key, (owners,), 0, 4)
    scores = jax.random.randint(score_key, (blocks, owners), 0, 16) * weight[None, :] * owners + jnp.arange(owners, dtype=jnp.int32)[None, :]
    chosen = jnp.argsort(scores, axis=1, stable=True)[:, :entries].astype(jnp.int32)
    local = jax.random.randint(row_key, (blocks, entries), 0, CH_DEV)
    slots = chosen * CH_DEV + local
    ids = span_at[slots].reshape(REQS, TOPK).astype(jnp.int32)
    return (slot_of, ids)


def draw_owner_slot(key, part):
    return retrieval_layout(key)[0]


def draw_span_ids(key, part):
    return retrieval_layout(key)[1]


def draw_recompute_rows(key, part):
    key = jax.random.fold_in(key, 7)
    scores = jax.random.randint(key, (SPANS, CLEN), 0, 2 ** 20) * CLEN + jnp.arange(CLEN, dtype=jnp.int32)[None, :]
    return jax.lax.top_k(scores, RROWS)[1].astype(jnp.int32)


def draw_queries(key, part):
    key = jax.random.fold_in(key, 11)
    shape = (LAYERS, REQS, QLEN, QH * HD)
    base = jnp.clip(1.4 * jax.random.normal(key, shape, jnp.float32), -5.0, 5.0)
    return base.astype(jnp.bfloat16)


def draw_query_keys(key, part):
    key = jax.random.fold_in(key, 13)
    shape = (LAYERS, REQS, QLEN, KVH * HD)
    base = jnp.clip(1.4 * jax.random.normal(key, shape, jnp.float32), -5.0, 5.0)
    return base.astype(jnp.bfloat16)


def steps_of(stream_key, extent, pieces, smallest, top_value):
    def one(axis_at, parts):
        steps = jax.random.uniform(jax.random.fold_in(jax.random.fold_in(stream_key, 6), axis_at), (parts,), jnp.float32, smallest / len(pieces), top_value / len(pieces))
        return jnp.repeat(jnp.exp(steps), extent[axis_at] // parts).reshape((-1,) + (1,) * (len(extent) - axis_at - 1))

    loudness = one(*pieces[0])
    for cut in pieces[1:]:
        loudness = loudness * one(*cut)
    return loudness


def centred(key, dims, scale, bound, pieces=(), held_as=jnp.bfloat16):
    array = jax.random.normal(key, dims, jnp.float32) * scale
    if len(pieces) > 0:
        array = steps_of(key, dims, pieces, -0.22, 0.18) * array
    return jnp.clip(array, min=-bound, max=bound).astype(held_as)


def setup_inputs(seed: int = 0) -> dict:
    arg_keys = jax.random.split(jax.random.key(seed), 12)
    return {
        "cache_keys": centred(arg_keys[0], (LAYERS, SPANS, CLEN, KVH * HD), 1.4, 5.0, ((1, 32), (3, 8))),
        "cache_values": centred(arg_keys[1], (LAYERS, SPANS, CLEN, KVH * HD), 1.0, 5.0, ((1, 32), (3, 8))),
        "span_ids": draw_span_ids(jax.random.fold_in(arg_keys[11], 71), 0),
        "owner_slot": draw_owner_slot(jax.random.fold_in(arg_keys[11], 71), 0),
        "recompute_rows": draw_recompute_rows(jax.random.fold_in(arg_keys[11], 71), 0),
        "hidden": centred(arg_keys[5], (LAYERS, REQS, TOPK, RROWS, D), 1.0, 6.0, ((0, 2), (1, 16), (4, 8))),
        "w_key": centred(arg_keys[6], (LAYERS, D, KVH * HD), D ** -0.5, 0.0625, ((0, 2), (1, 8))),
        "w_value": centred(arg_keys[7], (LAYERS, D, KVH * HD), D ** -0.5, 0.0625, ((0, 2), (1, 8))),
        "queries": draw_queries(jax.random.fold_in(arg_keys[11], 71), 0),
        "query_keys": draw_query_keys(jax.random.fold_in(arg_keys[11], 71), 0),
        "query_values": centred(arg_keys[10], (LAYERS, REQS, QLEN, KVH * HD), 1.0, 5.0, ((0, 2), (1, 16), (3, 8))),
    }


def attend(query_rows, keys, values):
    context = keys.shape[0] - QLEN
    group = QH // KVH
    qf = query_rows.astype(jnp.float32).reshape(QLEN, KVH, group, HD)
    kf = keys.astype(jnp.float32).reshape(-1, KVH, HD)
    vf = values.astype(jnp.float32).reshape(-1, KVH, HD)
    scores = jnp.einsum('qkgd,nkd->kgqn', qf, kf) / jnp.sqrt(jnp.float32(HD))
    col = jnp.arange(keys.shape[0], dtype=jnp.int32)[None, :]
    row = jnp.arange(QLEN, dtype=jnp.int32)[:, None]
    allowed = (col < context) | (col - context <= row)
    scores = jnp.where(allowed, scores, jnp.float32(-1e+30))
    top = lax.optimization_barrier(jnp.max(scores, axis=-1, keepdims=True))
    expo = jnp.exp(scores - top)
    probs = (expo / lax.optimization_barrier(jnp.sum(expo, axis=-1, keepdims=True))).astype(jnp.bfloat16)
    out = jnp.einsum('kgqn,nkd->qkgd', probs.astype(jnp.float32), vf)
    return out.reshape(QLEN, QH * HD).astype(jnp.bfloat16)

def project(rows, weight):
    block = D // N_TENSOR
    total = jnp.zeros((rows.shape[0], weight.shape[1]), jnp.float32)
    for part in range(N_TENSOR):
        piece = jnp.dot(rows[:, part * block:(part + 1) * block], weight[part * block:(part + 1) * block], preferred_element_type=jnp.float32)
        rounded = lax.optimization_barrier(piece.astype(jnp.bfloat16))
        total = total + rounded.astype(jnp.float32)
    return total.astype(jnp.bfloat16)

def reference(cache_keys, cache_values, span_ids, owner_slot, recompute_rows, hidden, w_key, w_value, queries, query_keys, query_values):
    width = KVH * HD
    results = []
    for layer in range(LAYERS):
        rows = hidden[layer].reshape(-1, D)
        new_keys = project(rows, w_key[layer]).reshape(REQS, TOPK, RROWS, width)
        new_values = project(rows, w_value[layer]).reshape(REQS, TOPK, RROWS, width)
        store_keys = cache_keys[layer]
        store_values = cache_values[layer]

        def one_request(items):
            ids, fresh_k, fresh_v, query_rows, own_k, own_v = items
            slots = owner_slot[ids].astype(jnp.int32)
            span_k = store_keys[slots].reshape(-1, width)
            span_v = store_values[slots].reshape(-1, width)
            picked = recompute_rows[ids].astype(jnp.int32)
            flat = (jnp.arange(TOPK, dtype=jnp.int32)[:, None] * CLEN + picked).reshape(-1)
            span_k = span_k.at[flat].set(fresh_k.reshape(-1, width))
            span_v = span_v.at[flat].set(fresh_v.reshape(-1, width))
            keys = jnp.concatenate([span_k, own_k], axis=0)
            values = jnp.concatenate([span_v, own_v], axis=0)
            return attend(query_rows, keys, values)
        results.append(lax.map(one_request, (span_ids, new_keys, new_values, queries[layer], query_keys[layer], query_values[layer])))
    return jnp.stack(results)
```

```python
import functools

import jax
import jax.numpy as jnp
from jax import lax
from jax.experimental import pallas as pl
from jax.experimental.pallas import tpu as pltpu
from jax.sharding import PartitionSpec as P

HD = 128
TILE = 16
MIB = 1 << 20
LOG2E = 1.4426950408889634


def ceil_to(n, m):
    return -(-n // m) * m


def compact_kernel(ids_ref, rows_ref, ck_ref, cv_ref, out_ref, *, kept):
    layers, _, clen, width = ck_ref.shape
    padded = out_ref.shape[2]
    rr = rows_ref.shape[1]
    rows = rows_ref[pl.ds(lax.rem(ids_ref[pl.program_id(0)], 8), 1), :]
    hit = (lax.broadcasted_iota(jnp.int32, (clen, rr), 0) == rows).astype(jnp.bfloat16)
    gone = lax.dot_general(
        jnp.ones((8, rr), jnp.bfloat16), hit, (((1,), (1,)), ((), ())),
        preferred_element_type=jnp.float32,
    )
    keep = 1.0 - gone
    earlier = (
        lax.broadcasted_iota(jnp.int32, (clen, clen), 0)
        < lax.broadcasted_iota(jnp.int32, (clen, clen), 1)
    ).astype(jnp.bfloat16)
    rank = jnp.dot(keep.astype(jnp.bfloat16), earlier, preferred_element_type=jnp.float32)[:1]
    rank = jnp.where(keep[:1] > 0.5, rank.astype(jnp.int32), -1)
    target = lax.broadcasted_iota(jnp.int32, (padded, clen), 0)
    target = jnp.where(target < kept, target, 0)
    pick = (target == rank).astype(jnp.bfloat16)
    for layer in range(layers):
        both = jnp.concatenate([ck_ref[layer, 0], cv_ref[layer, 0]], axis=1)
        out_ref[layer, 0] = jnp.dot(
            pick, both, preferred_element_type=jnp.float32
        ).astype(out_ref.dtype)


def compact(ids, recompute_rows, cache_keys, cache_values, kept, padded):
    layers, spans, clen, width = cache_keys.shape
    rr = recompute_rows.shape[1]
    return pl.pallas_call(
        functools.partial(compact_kernel, kept=kept),
        grid_spec=pltpu.PrefetchScalarGridSpec(
            num_scalar_prefetch=1,
            grid=(spans,),
            in_specs=[
                pl.BlockSpec((8, rr), lambda i, ids: (ids[i] // 8, 0)),
                pl.BlockSpec((layers, 1, clen, width), lambda i, ids: (0, i, 0, 0)),
                pl.BlockSpec((layers, 1, clen, width), lambda i, ids: (0, i, 0, 0)),
            ],
            out_specs=pl.BlockSpec((layers, 1, padded, 2 * width), lambda i, ids: (0, i, 0, 0)),
        ),
        out_shape=jax.ShapeDtypeStruct((layers, spans, padded, 2 * width), jnp.bfloat16),
        compiler_params=pltpu.CompilerParams(vmem_limit_bytes=56 * MIB),
        cost_estimate=pl.CostEstimate(
            flops=2 * layers * spans * padded * clen * 2 * width,
            bytes_accessed=8 * layers * spans * clen * width,
            transcendentals=0,
        ),
        name="compact",
    )(ids, recompute_rows, cache_keys, cache_values)


def spread_kernel(local_ref, packed_ref, main_ref, rest_ref, sem, *, groups, cut):
    layers, _, padded, _ = packed_ref.shape

    def copies(g):
        made = []
        for layer in range(layers):
            dest = layer * groups + g
            made.append(
                pltpu.make_async_copy(
                    packed_ref.at[layer, local_ref[g], pl.ds(0, cut)],
                    main_ref.at[dest],
                    sem.at[0, dest],
                )
            )
            made.append(
                pltpu.make_async_copy(
                    packed_ref.at[layer, local_ref[g], pl.ds(cut, padded - cut)],
                    rest_ref.at[dest],
                    sem.at[1, dest],
                )
            )
        return made

    for g in range(groups):

        @pl.when(local_ref[g] >= 0)
        def _():
            for copy in copies(g):
                copy.start()

    for g in range(groups):

        @pl.when(local_ref[g] >= 0)
        def _():
            for copy in copies(g):
                copy.wait()


def spread(local, packed, cut):
    layers, spans, padded, wide = packed.shape
    groups = local.shape[0]
    dests = layers * groups
    return pl.pallas_call(
        functools.partial(spread_kernel, groups=groups, cut=cut),
        in_specs=[
            pl.BlockSpec(memory_space=pltpu.SMEM),
            pl.BlockSpec(memory_space=pltpu.VMEM),
        ],
        out_specs=[pl.BlockSpec(memory_space=pl.ANY), pl.BlockSpec(memory_space=pl.ANY)],
        out_shape=[
            jax.ShapeDtypeStruct((dests, cut, wide), jnp.bfloat16),
            jax.ShapeDtypeStruct((dests, padded - cut, wide), jnp.bfloat16),
        ],
        scratch_shapes=[pltpu.SemaphoreType.DMA((2, dests))],
        compiler_params=pltpu.CompilerParams(vmem_limit_bytes=56 * MIB),
        cost_estimate=pl.CostEstimate(
            flops=0, bytes_accessed=2 * (dests + layers * spans) * padded * wide, transcendentals=0
        ),
        name="spread",
    )(local, packed)


def project_kernel(hidden_ref, wk_ref, wv_ref, out_ref, rows_ref, *, rrows, slot):
    _, reqs, topk, _, _ = hidden_ref.shape

    @pl.when(pl.program_id(0) == 0)
    def _():
        for r in range(reqs):
            for j in range(topk):
                at = (r * topk + j) * slot
                rows_ref[at : at + rrows] = hidden_ref[0, r, j]
                if slot > rrows:
                    rows_ref[at + rrows : at + slot] = hidden_ref[0, r, j, : slot - rrows]

    weight = jnp.concatenate([wk_ref[0], wv_ref[0]], axis=1)
    out_ref[0] = jnp.dot(
        rows_ref[...], weight, preferred_element_type=jnp.float32
    ).astype(out_ref.dtype)


def project(hidden, w_key, w_value, slot, parts):
    _, reqs, topk, rrows, feats = hidden.shape
    spans = reqs * topk
    share = w_key.shape[2] // parts
    return pl.pallas_call(
        functools.partial(project_kernel, rrows=rrows, slot=slot),
        grid=(parts,),
        in_specs=[
            pl.BlockSpec(hidden.shape, lambda p: (0, 0, 0, 0, 0)),
            pl.BlockSpec((1, feats, share), lambda p: (0, 0, p)),
            pl.BlockSpec((1, feats, share), lambda p: (0, 0, p)),
        ],
        out_specs=pl.BlockSpec((1, spans * slot, 2 * share), lambda p: (p, 0, 0)),
        out_shape=jax.ShapeDtypeStruct((parts, spans * slot, 2 * share), jnp.bfloat16),
        scratch_shapes=[pltpu.VMEM((spans * slot, feats), jnp.bfloat16)],
        compiler_params=pltpu.CompilerParams(vmem_limit_bytes=56 * MIB),
        cost_estimate=pl.CostEstimate(
            flops=4 * parts * spans * slot * feats * share,
            bytes_accessed=2 * spans * rrows * feats + 4 * parts * (feats + spans * slot) * share,
            transcendentals=0,
        ),
        name="project",
    )(hidden, w_key, w_value)


def attend_step(q_ref, key_ref, wide_ref, acc_ref, top_ref, first, causal):
    heads = acc_ref.shape[0]
    qlen = acc_ref.shape[1]
    count = key_ref.shape[0]
    factor = LOG2E / (HD ** 0.5)

    def one_head(h):
        q = q_ref[:, h * HD : (h + 1) * HD]
        scores = lax.dot_general(
            q, key_ref[...], (((1,), (1,)), ((), ())), preferred_element_type=jnp.float32
        )
        if causal is not None:
            scores = jnp.concatenate(
                [scores[:, : count - qlen], jnp.where(causal, scores[:, count - qlen :], -1e30)],
                axis=1,
            )
        best = jnp.max(scores, axis=1, keepdims=True) * factor
        if first:
            top = best
        else:
            old = top_ref[h][:, :1]
            top = jnp.maximum(old, best)
        probs = jnp.exp2(scores * factor - top).astype(jnp.bfloat16)
        part = jnp.dot(probs, wide_ref[...], preferred_element_type=jnp.float32)
        if first:
            acc_ref[h] = part
        else:
            acc_ref[h] = acc_ref[h] * jnp.exp2(old - top) + part
        top_ref[h] = jnp.broadcast_to(top, (qlen, HD))

    for h in range(heads):
        one_head(h)


def gather_keys(blocks, key_ref, wide_ref, at, kept):
    rows = blocks[0].shape[1]
    real = lax.broadcasted_iota(jnp.int32, (rows, HD), 0) < kept
    for ref in blocks:
        key_ref[at : at + rows] = ref[0, :, :HD]
        value = ref[0, :, HD:]
        if kept < rows:
            value = jnp.where(real, value, 0).astype(jnp.bfloat16)
        wide_ref[at : at + rows, :HD] = value
        wide_ref[at : at + rows, HD:] = real.astype(jnp.bfloat16)
        at += rows


def main_kernel(place_ref, q_ref, fresh_ref, nk_ref, nv_ref, *rest, rrows, slot):
    acc_ref, top_ref, key_ref, wide_ref = rest[-4:]
    blocks = rest[:-4]
    rows = blocks[0].shape[1]
    fresh_rows = fresh_ref.shape[0]
    qlen = nk_ref.shape[2]
    gather_keys(blocks, key_ref, wide_ref, 0, rows)
    at = rows * len(blocks)
    end = at + fresh_rows
    real = lax.broadcasted_iota(jnp.int32, (fresh_rows, HD), 0) % slot < rrows
    key_ref[at:end] = fresh_ref[:, :HD]
    wide_ref[at:end, :HD] = jnp.where(real, fresh_ref[:, HD:], 0).astype(jnp.bfloat16)
    wide_ref[at:end, HD:] = real.astype(jnp.bfloat16)
    key_ref[end:] = nk_ref[0, 0]
    wide_ref[end:, :HD] = nv_ref[0, 0]
    wide_ref[end:, HD:] = jnp.ones((qlen, HD), jnp.bfloat16)
    causal = lax.broadcasted_iota(jnp.int32, (qlen, qlen), 0) >= lax.broadcasted_iota(
        jnp.int32, (qlen, qlen), 1
    )
    attend_step(q_ref.at[0, 0], key_ref, wide_ref, acc_ref.at[0], top_ref.at[0], True, causal)


def block_specs(rows, topk):
    return [
        pl.BlockSpec((1, rows, 2 * HD), lambda r, at, j=j: (at[r * topk + j], 0, 0))
        for j in range(topk)
    ]


def attend_main(place, queries, fresh, query_keys, query_values, arrived, rrows, slot):
    _, reqs, qlen, feats = queries.shape
    heads = feats // HD
    rows = arrived.shape[1]
    topk = place.shape[0] // reqs
    fresh_rows = fresh.shape[0] // reqs
    count = topk * rows + fresh_rows + qlen
    return pl.pallas_call(
        functools.partial(main_kernel, rrows=rrows, slot=slot),
        grid_spec=pltpu.PrefetchScalarGridSpec(
            num_scalar_prefetch=1,
            grid=(reqs,),
            in_specs=[
                pl.BlockSpec((1, 1, qlen, feats), lambda r, at: (0, r, 0, 0)),
                pl.BlockSpec((fresh_rows, 2 * HD), lambda r, at: (r, 0)),
                pl.BlockSpec((1, 1, qlen, HD), lambda r, at: (0, r, 0, 0)),
                pl.BlockSpec((1, 1, qlen, HD), lambda r, at: (0, r, 0, 0)),
            ]
            + block_specs(rows, topk),
            out_specs=[
                pl.BlockSpec((1, heads, qlen, 2 * HD), lambda r, at: (r, 0, 0, 0)),
                pl.BlockSpec((1, heads, qlen, HD), lambda r, at: (r, 0, 0, 0)),
            ],
            scratch_shapes=[
                pltpu.VMEM((count, HD), jnp.bfloat16),
                pltpu.VMEM((count, 2 * HD), jnp.bfloat16),
            ],
        ),
        out_shape=[
            jax.ShapeDtypeStruct((reqs, heads, qlen, 2 * HD), jnp.float32),
            jax.ShapeDtypeStruct((reqs, heads, qlen, HD), jnp.float32),
        ],
        compiler_params=pltpu.CompilerParams(vmem_limit_bytes=56 * MIB),
        cost_estimate=pl.CostEstimate(
            flops=6 * reqs * heads * qlen * count * HD,
            bytes_accessed=4 * reqs * count * HD + 12 * reqs * heads * qlen * HD,
            transcendentals=reqs * heads * qlen * count,
        ),
        name="attend_main",
    )(place, queries, fresh, query_keys, query_values, *([arrived] * topk))


def last_kernel(place_ref, q_ref, acc_in, top_in, *rest, kept):
    out_ref, acc_ref, top_ref, key_ref, wide_ref = rest[-5:]
    gather_keys(rest[:-5], key_ref, wide_ref, 0, kept)
    acc_ref[...] = acc_in[0]
    top_ref[...] = top_in[0]
    attend_step(q_ref.at[0, 0], key_ref, wide_ref, acc_ref, top_ref, False, None)
    for h in range(acc_ref.shape[0]):
        total = acc_ref[h]
        out_ref[0, 0, :, h * HD : (h + 1) * HD] = (total[:, :HD] / total[:, HD:]).astype(
            out_ref.dtype
        )


def attend_last(place, queries, acc, top, arrived, kept):
    _, reqs, qlen, feats = queries.shape
    heads = feats // HD
    rows = arrived.shape[1]
    topk = place.shape[0] // reqs
    count = topk * rows
    return pl.pallas_call(
        functools.partial(last_kernel, kept=kept),
        grid_spec=pltpu.PrefetchScalarGridSpec(
            num_scalar_prefetch=1,
            grid=(reqs,),
            in_specs=[
                pl.BlockSpec((1, 1, qlen, feats), lambda r, at: (0, r, 0, 0)),
                pl.BlockSpec((1, heads, qlen, 2 * HD), lambda r, at: (r, 0, 0, 0)),
                pl.BlockSpec((1, heads, qlen, HD), lambda r, at: (r, 0, 0, 0)),
            ]
            + block_specs(rows, topk),
            out_specs=pl.BlockSpec((1, 1, qlen, feats), lambda r, at: (0, r, 0, 0)),
            scratch_shapes=[
                pltpu.VMEM((heads, qlen, 2 * HD), jnp.float32),
                pltpu.VMEM((heads, qlen, HD), jnp.float32),
                pltpu.VMEM((count, HD), jnp.bfloat16),
                pltpu.VMEM((count, 2 * HD), jnp.bfloat16),
            ],
        ),
        out_shape=jax.ShapeDtypeStruct(queries.shape, jnp.bfloat16),
        compiler_params=pltpu.CompilerParams(vmem_limit_bytes=56 * MIB),
        cost_estimate=pl.CostEstimate(
            flops=6 * reqs * heads * qlen * count * HD,
            bytes_accessed=4 * reqs * count * HD + 12 * reqs * heads * qlen * HD,
            transcendentals=reqs * heads * qlen * count,
        ),
        name="attend_last",
    )(place, queries, acc, top, *([arrived] * topk))


def on_device(
    cache_keys,
    cache_values,
    span_ids,
    owner_slot,
    recompute_rows,
    hidden,
    w_key,
    w_value,
    queries,
    query_keys,
    query_values,
):
    sections = lax.axis_size("section")
    groups = lax.axis_size("dp")
    parts = lax.axis_size("tensor")
    per_owner = cache_keys.shape[1]
    clen = cache_keys.shape[2]
    req_dev, topk = span_ids.shape
    rrows = hidden.shape[3]
    kept = clen - rrows
    cut = kept // HD * HD
    padded = ceil_to(kept, 64)
    slot = ceil_to(rrows, TILE)
    myself = lax.axis_index("section") * groups + lax.axis_index("dp")

    own_slot = owner_slot[span_ids].reshape(req_dev * topk)
    every_slot = lax.all_to_all(
        jnp.broadcast_to(own_slot[None], (groups, req_dev * topk)), "dp", 0, 0
    )

    here = myself * per_owner + jnp.arange(per_owner, dtype=jnp.int32)
    held = owner_slot[None, :] == here[:, None]
    ids = jnp.sum(
        jnp.where(held, jnp.arange(owner_slot.shape[0], dtype=jnp.int32)[None], 0), axis=1
    )
    packed = compact(ids, recompute_rows, cache_keys, cache_values, kept, padded)

    partial = project(hidden, w_key, w_value, slot, parts)

    mine = every_slot // per_owner == myself
    local = jnp.max(jnp.where(mine, every_slot % per_owner, -1), axis=1)
    main, rest = spread(local, packed, cut)
    arrived = lax.all_to_all(main, ("section", "dp"), 0, 0, tiled=True)
    fresh = lax.psum_scatter(
        partial.reshape(parts * req_dev * topk * slot, -1),
        "tensor",
        scatter_dimension=0,
        tiled=True,
    )
    rest, arrived = lax.optimization_barrier((rest, arrived))
    arrived_rest = lax.all_to_all(rest, ("section", "dp"), 0, 0, tiled=True)

    place = own_slot // per_owner
    acc, top = attend_main(
        place, queries, fresh, query_keys, query_values, arrived, rrows, slot
    )
    return attend_last(place, queries, acc, top, arrived_rest, kept - cut)


def solution(mesh):
    in_specs = (
        P(None, ("section", "dp"), None, "tensor"),
        P(None, ("section", "dp"), None, "tensor"),
        P("dp", None),
        P(),
        P(),
        P("section", "dp", None, None, "tensor"),
        P("section", "tensor", None),
        P("section", "tensor", None),
        P("section", "dp", None, "tensor"),
        P("section", "dp", None, "tensor"),
        P("section", "dp", None, "tensor"),
    )
    out_specs = P("section", "dp", None, "tensor")
    return jax.shard_map(
        on_device, mesh=mesh, in_specs=in_specs, out_specs=out_specs, check_vma=False
    )
```

```python
import functools

import jax
import jax.numpy as jnp
from jax import lax
from jax.experimental import pallas as pl
from jax.experimental.pallas import tpu as pltpu
from jax.sharding import PartitionSpec as P

HD = 128
TILE = 16
MIB = 1 << 20
LOG2E = 1.4426950408889634


def ceil_to(n, m):
    return -(-n // m) * m


def compact_kernel(ids_ref, rows_ref, ck_ref, cv_ref, out_ref, *, kept):
    layers, some, clen, width = ck_ref.shape
    padded = out_ref.shape[2]
    rr = rows_ref.shape[1]
    earlier = (
        lax.broadcasted_iota(jnp.int32, (clen, clen), 0)
        < lax.broadcasted_iota(jnp.int32, (clen, clen), 1)
    ).astype(jnp.bfloat16)
    ones = jnp.ones((8, rr), jnp.bfloat16)
    target = lax.broadcasted_iota(jnp.int32, (padded, clen), 0)
    target = jnp.where(target < kept, target, 0)
    keeps = []
    for i in range(some):
        rows = rows_ref[pl.ds(ids_ref[pl.program_id(0) * some + i], 1), :]
        hit = (lax.broadcasted_iota(jnp.int32, (clen, rr), 0) == rows).astype(jnp.bfloat16)
        gone = lax.dot_general(
            ones, hit, (((1,), (1,)), ((), ())), preferred_element_type=jnp.float32
        )
        keeps.append(1.0 - gone)
    ranks = jnp.dot(
        jnp.concatenate(keeps, axis=0).astype(jnp.bfloat16),
        earlier,
        preferred_element_type=jnp.float32,
    )
    for i in range(some):
        rank = ranks[8 * i : 8 * i + 1].astype(jnp.int32)
        rank = jnp.where(keeps[i][:1] > 0.5, rank, -1)
        pick = (target == rank).astype(jnp.bfloat16)
        for layer in range(layers):
            both = jnp.concatenate([ck_ref[layer, i], cv_ref[layer, i]], axis=1)
            out_ref[layer, i] = jnp.dot(
                pick, both, preferred_element_type=jnp.float32
            ).astype(out_ref.dtype)


def compact(ids, recompute_rows, cache_keys, cache_values, kept, padded):
    layers, spans, clen, width = cache_keys.shape
    some = spans // 2
    cache_spec = pl.BlockSpec((layers, some, clen, width), lambda i, ids: (0, i, 0, 0))
    return pl.pallas_call(
        functools.partial(compact_kernel, kept=kept),
        grid_spec=pltpu.PrefetchScalarGridSpec(
            num_scalar_prefetch=1,
            grid=(spans // some,),
            in_specs=[
                pl.BlockSpec(recompute_rows.shape, lambda i, ids: (0, 0)),
                cache_spec,
                cache_spec,
            ],
            out_specs=pl.BlockSpec(
                (layers, some, padded, 2 * width), lambda i, ids: (0, i, 0, 0)
            ),
        ),
        out_shape=jax.ShapeDtypeStruct((layers, spans, padded, 2 * width), jnp.bfloat16),
        compiler_params=pltpu.CompilerParams(vmem_limit_bytes=56 * MIB),
        cost_estimate=pl.CostEstimate(
            flops=2 * layers * spans * padded * clen * 2 * width,
            bytes_accessed=8 * layers * spans * clen * width,
            transcendentals=0,
        ),
        name="compact",
    )(ids, recompute_rows, cache_keys, cache_values)


def spread_kernel(local_ref, packed_ref, main_ref, rest_ref, sem, *, groups, cut):
    layers, _, padded, _ = packed_ref.shape

    def copies(g):
        made = []
        for layer in range(layers):
            dest = layer * groups + g
            made.append(
                pltpu.make_async_copy(
                    packed_ref.at[layer, local_ref[g], pl.ds(0, cut)],
                    main_ref.at[dest],
                    sem.at[0, dest],
                )
            )
            made.append(
                pltpu.make_async_copy(
                    packed_ref.at[layer, local_ref[g], pl.ds(cut, padded - cut)],
                    rest_ref.at[dest],
                    sem.at[1, dest],
                )
            )
        return made

    for g in range(groups):

        @pl.when(local_ref[g] >= 0)
        def _():
            for copy in copies(g):
                copy.start()

    for g in range(groups):

        @pl.when(local_ref[g] >= 0)
        def _():
            for copy in copies(g):
                copy.wait()


def spread(local, packed, cut):
    layers, spans, padded, wide = packed.shape
    groups = local.shape[0]
    dests = layers * groups
    return pl.pallas_call(
        functools.partial(spread_kernel, groups=groups, cut=cut),
        in_specs=[
            pl.BlockSpec(memory_space=pltpu.SMEM),
            pl.BlockSpec(memory_space=pltpu.VMEM),
        ],
        out_specs=[pl.BlockSpec(memory_space=pl.ANY), pl.BlockSpec(memory_space=pl.ANY)],
        out_shape=[
            jax.ShapeDtypeStruct((dests, cut, wide), jnp.bfloat16),
            jax.ShapeDtypeStruct((dests, padded - cut, wide), jnp.bfloat16),
        ],
        scratch_shapes=[pltpu.SemaphoreType.DMA((2, dests))],
        compiler_params=pltpu.CompilerParams(vmem_limit_bytes=56 * MIB),
        cost_estimate=pl.CostEstimate(
            flops=0, bytes_accessed=2 * (dests + layers * spans) * padded * wide, transcendentals=0
        ),
        name="spread",
    )(local, packed)


def project_kernel(hidden_ref, wk_ref, wv_ref, out_ref, rows_ref, *, rrows, slot):
    _, reqs, topk, _, _ = hidden_ref.shape

    @pl.when(pl.program_id(0) == 0)
    def _():
        for r in range(reqs):
            for j in range(topk):
                at = (r * topk + j) * slot
                rows_ref[at : at + rrows] = hidden_ref[0, r, j]
                if slot > rrows:
                    rows_ref[at + rrows : at + slot] = hidden_ref[0, r, j, : slot - rrows]

    weight = jnp.concatenate([wk_ref[0], wv_ref[0]], axis=1)
    out_ref[0] = jnp.dot(
        rows_ref[...], weight, preferred_element_type=jnp.float32
    ).astype(out_ref.dtype)


def project(hidden, w_key, w_value, slot, parts):
    _, reqs, topk, rrows, feats = hidden.shape
    spans = reqs * topk
    share = w_key.shape[2] // parts
    return pl.pallas_call(
        functools.partial(project_kernel, rrows=rrows, slot=slot),
        grid=(parts,),
        in_specs=[
            pl.BlockSpec(hidden.shape, lambda p: (0, 0, 0, 0, 0)),
            pl.BlockSpec((1, feats, share), lambda p: (0, 0, p)),
            pl.BlockSpec((1, feats, share), lambda p: (0, 0, p)),
        ],
        out_specs=pl.BlockSpec((1, spans * slot, 2 * share), lambda p: (p, 0, 0)),
        out_shape=jax.ShapeDtypeStruct((parts, spans * slot, 2 * share), jnp.bfloat16),
        scratch_shapes=[pltpu.VMEM((spans * slot, feats), jnp.bfloat16)],
        compiler_params=pltpu.CompilerParams(vmem_limit_bytes=56 * MIB),
        cost_estimate=pl.CostEstimate(
            flops=4 * parts * spans * slot * feats * share,
            bytes_accessed=2 * spans * rrows * feats + 4 * parts * (feats + spans * slot) * share,
            transcendentals=0,
        ),
        name="project",
    )(hidden, w_key, w_value)


def attend_head(q, key_ref, wide_ref, state, causal):
    qlen = q.shape[0]
    count = key_ref.shape[0]
    factor = LOG2E / (HD ** 0.5)
    scores = lax.dot_general(
        q, key_ref[...], (((1,), (1,)), ((), ())), preferred_element_type=jnp.float32
    )
    if causal is not None:
        scores = jnp.concatenate(
            [scores[:, : count - qlen], jnp.where(causal, scores[:, count - qlen :], -1e30)],
            axis=1,
        )
    top = jnp.max(scores, axis=1, keepdims=True) * factor
    if state is not None:
        old = state[:, 2 * HD - 1 :]
        top = jnp.maximum(old, top)
    probs = jnp.exp2(scores * factor - top).astype(jnp.bfloat16)
    total = jnp.dot(probs, wide_ref[...], preferred_element_type=jnp.float32)
    if state is not None:
        total = total + state * jnp.exp2(old - top)
    return total, top


def pack_state(total, top):
    lane = lax.broadcasted_iota(jnp.int32, total.shape, 1)
    return jnp.where(lane < 2 * HD - HD // 2, total, top)


def gather_keys(blocks, key_ref, wide_ref, kept):
    rows = blocks[0].shape[1]
    real = lax.broadcasted_iota(jnp.int32, (rows, HD), 0) < kept
    for j, ref in enumerate(blocks):
        span = slice(j * rows, (j + 1) * rows)
        key_ref[span] = ref[0, :, :HD]
        value = ref[0, :, HD:]
        if kept < rows:
            value = jnp.where(real, value, 0).astype(jnp.bfloat16)
        wide_ref[span, :HD] = value
        wide_ref[span, HD:] = real.astype(jnp.bfloat16)


def own_kernel(
    q_ref, half_ref, other_ref, nk_ref, nv_ref, out_ref, key_ref, wide_ref, *, rrows, slot
):
    fresh_rows = half_ref.shape[0]
    qlen = nk_ref.shape[2]

    @pl.when(pl.program_id(1) == 0)
    def _():
        real = lax.broadcasted_iota(jnp.int32, (fresh_rows, HD), 0) % slot < rrows
        fresh = half_ref[...].astype(jnp.float32) + other_ref[...].astype(jnp.float32)
        key_ref[:fresh_rows] = fresh[:, :HD].astype(jnp.bfloat16)
        wide_ref[:fresh_rows, :HD] = jnp.where(real, fresh[:, HD:], 0).astype(jnp.bfloat16)
        wide_ref[:fresh_rows, HD:] = real.astype(jnp.bfloat16)
        key_ref[fresh_rows:] = nk_ref[0, 0]
        wide_ref[fresh_rows:, :HD] = nv_ref[0, 0]
        wide_ref[fresh_rows:, HD:] = jnp.ones((qlen, HD), jnp.bfloat16)

    causal = lax.broadcasted_iota(jnp.int32, (qlen, qlen), 0) >= lax.broadcasted_iota(
        jnp.int32, (qlen, qlen), 1
    )
    for h in range(out_ref.shape[1]):
        q = q_ref[0, 0, :, h * HD : (h + 1) * HD]
        out_ref[0, h] = pack_state(*attend_head(q, key_ref, wide_ref, None, causal))


def main_kernel(place_ref, q_ref, state_ref, *rest):
    out_ref, key_ref, wide_ref = rest[-3:]
    blocks = rest[:-3]

    @pl.when(pl.program_id(1) == 0)
    def _():
        gather_keys(blocks, key_ref, wide_ref, blocks[0].shape[1])

    for h in range(out_ref.shape[1]):
        q = q_ref[0, 0, :, h * HD : (h + 1) * HD]
        out_ref[0, h] = pack_state(*attend_head(q, key_ref, wide_ref, state_ref[0, h], None))


def last_kernel(place_ref, q_ref, state_ref, *rest, kept):
    out_ref, key_ref, wide_ref = rest[-3:]
    blocks = rest[:-3]

    @pl.when(pl.program_id(1) == 0)
    def _():
        gather_keys(blocks, key_ref, wide_ref, kept)

    for h in range(state_ref.shape[1]):
        lanes = slice(h * HD, (h + 1) * HD)
        total, _ = attend_head(
            q_ref[0, 0, :, lanes], key_ref, wide_ref, state_ref[0, h], None
        )
        out_ref[0, 0, :, lanes] = (total[:, :HD] / total[:, HD : HD + 1]).astype(out_ref.dtype)


def attend_cost(reqs, heads, qlen, count):
    return pl.CostEstimate(
        flops=6 * reqs * heads * qlen * count * HD,
        bytes_accessed=4 * reqs * count * HD + 16 * reqs * heads * qlen * HD,
        transcendentals=reqs * heads * qlen * count,
    )


def attend_own(queries, half, other, query_keys, query_values, rrows, slot):
    _, reqs, qlen, feats = queries.shape
    heads = feats // HD
    some = heads // 2
    fresh_rows = half.shape[0] // reqs
    count = fresh_rows + qlen
    return pl.pallas_call(
        functools.partial(own_kernel, rrows=rrows, slot=slot),
        grid=(reqs, heads // some),
        in_specs=[
            pl.BlockSpec((1, 1, qlen, some * HD), lambda r, h: (0, r, 0, h)),
            pl.BlockSpec((fresh_rows, 2 * HD), lambda r, h: (r, 0)),
            pl.BlockSpec((fresh_rows, 2 * HD), lambda r, h: (r, 0)),
            pl.BlockSpec((1, 1, qlen, HD), lambda r, h: (0, r, 0, 0)),
            pl.BlockSpec((1, 1, qlen, HD), lambda r, h: (0, r, 0, 0)),
        ],
        out_specs=pl.BlockSpec((1, some, qlen, 2 * HD), lambda r, h: (r, h, 0, 0)),
        out_shape=jax.ShapeDtypeStruct((reqs, heads, qlen, 2 * HD), jnp.float32),
        scratch_shapes=[
            pltpu.VMEM((count, HD), jnp.bfloat16),
            pltpu.VMEM((count, 2 * HD), jnp.bfloat16),
        ],
        compiler_params=pltpu.CompilerParams(vmem_limit_bytes=56 * MIB),
        cost_estimate=attend_cost(reqs, heads, qlen, count),
        name="attend_own",
    )(queries, half, other, query_keys, query_values)


def attend_spans(place, queries, state, arrived, kept, last):
    _, reqs, qlen, feats = queries.shape
    heads = feats // HD
    some = heads
    rows = arrived.shape[1]
    topk = place.shape[0] // reqs
    count = topk * rows
    q_spec = pl.BlockSpec((1, 1, qlen, some * HD), lambda r, h, at: (0, r, 0, h))
    state_spec = pl.BlockSpec((1, some, qlen, 2 * HD), lambda r, h, at: (r, h, 0, 0))
    blocks = [
        pl.BlockSpec((1, rows, 2 * HD), lambda r, h, at, j=j: (at[r * topk + j], 0, 0))
        for j in range(topk)
    ]
    return pl.pallas_call(
        functools.partial(last_kernel, kept=kept) if last else main_kernel,
        grid_spec=pltpu.PrefetchScalarGridSpec(
            num_scalar_prefetch=1,
            grid=(reqs, heads // some),
            in_specs=[q_spec, state_spec] + blocks,
            out_specs=q_spec if last else state_spec,
            scratch_shapes=[
                pltpu.VMEM((count, HD), jnp.bfloat16),
                pltpu.VMEM((count, 2 * HD), jnp.bfloat16),
            ],
        ),
        out_shape=jax.ShapeDtypeStruct(queries.shape, jnp.bfloat16)
        if last
        else jax.ShapeDtypeStruct(state.shape, state.dtype),
        compiler_params=pltpu.CompilerParams(vmem_limit_bytes=56 * MIB),
        cost_estimate=attend_cost(reqs, heads, qlen, count),
        name="attend_last" if last else "attend_main",
    )(place, queries, state, *([arrived] * topk))


def on_device(
    cache_keys,
    cache_values,
    span_ids,
    owner_slot,
    recompute_rows,
    hidden,
    w_key,
    w_value,
    queries,
    query_keys,
    query_values,
):
    sections = lax.axis_size("section")
    groups = lax.axis_size("dp")
    parts = lax.axis_size("tensor")
    per_owner = cache_keys.shape[1]
    clen = cache_keys.shape[2]
    req_dev, topk = span_ids.shape
    rrows = hidden.shape[3]
    kept = clen - rrows
    cut = kept // HD * HD
    padded = ceil_to(kept, 64)
    slot = ceil_to(rrows, TILE)
    myself = lax.axis_index("section") * groups + lax.axis_index("dp")

    own_slot = owner_slot[span_ids].reshape(req_dev * topk)
    every_slot = lax.all_to_all(
        jnp.broadcast_to(own_slot[None], (groups, req_dev * topk)), "dp", 0, 0
    )

    here = myself * per_owner + jnp.arange(per_owner, dtype=jnp.int32)
    held = owner_slot[None, :] == here[:, None]
    ids = jnp.sum(
        jnp.where(held, jnp.arange(owner_slot.shape[0], dtype=jnp.int32)[None], 0), axis=1
    )
    packed = compact(ids, recompute_rows, cache_keys, cache_values, kept, padded)

    mine = every_slot // per_owner == myself
    local = jnp.max(jnp.where(mine, every_slot % per_owner, -1), axis=1)
    main, rest = spread(local, packed, cut)
    main, hidden = lax.optimization_barrier((main, hidden))
    partial = project(hidden, w_key, w_value, slot, parts)
    arrived = lax.all_to_all(main, ("section", "dp"), 0, 0, tiled=True)
    outer = parts // 2
    along_y = [[2 * y + x for y in range(outer)] for x in range(2)]
    fresh = lax.psum_scatter(
        partial.reshape(parts * req_dev * topk * slot, -1),
        "tensor",
        scatter_dimension=0,
        tiled=True,
        axis_index_groups=along_y,
    ).reshape(2, req_dev * topk * slot, -1)
    side = lax.axis_index("tensor") % 2
    mine_half = lax.dynamic_index_in_dim(fresh, side, 0, keepdims=False)
    their_half = lax.dynamic_index_in_dim(fresh, 1 - side, 0, keepdims=False)
    other_half = lax.ppermute(their_half, "tensor", [(i, i ^ 1) for i in range(parts)])
    state = attend_own(
        queries, mine_half, other_half, query_keys, query_values, rrows, slot
    )
    rest, arrived, state = lax.optimization_barrier((rest, arrived, state))
    arrived_rest = lax.all_to_all(rest, ("section", "dp"), 0, 0, tiled=True)

    place = own_slot // per_owner
    state = attend_spans(place, queries, state, arrived, cut, False)
    return attend_spans(place, queries, state, arrived_rest, kept - cut, True)


def solution(mesh):
    in_specs = (
        P(None, ("section", "dp"), None, "tensor"),
        P(None, ("section", "dp"), None, "tensor"),
        P("dp", None),
        P(),
        P(),
        P("section", "dp", None, None, "tensor"),
        P("section", "tensor", None),
        P("section", "tensor", None),
        P("section", "dp", None, "tensor"),
        P("section", "dp", None, "tensor"),
        P("section", "dp", None, "tensor"),
    )
    out_specs = P("section", "dp", None, "tensor")
    return jax.shard_map(
        on_device, mesh=mesh, in_specs=in_specs, out_specs=out_specs, check_vma=False
    )
```

```python
import functools

import jax
import jax.numpy as jnp
from jax import lax
from jax.experimental import pallas as pl
from jax.experimental.pallas import tpu as pltpu
from jax.sharding import PartitionSpec as P

HD = 128
TILE = 16
MIB = 1 << 20
LOG2E = 1.4426950408889634


def ceil_to(n, m):
    return -(-n // m) * m


def compact_kernel(ids_ref, rows_ref, ck_ref, cv_ref, out_ref, *, kept):
    layers, some, clen, width = ck_ref.shape
    padded = out_ref.shape[2]
    rr = rows_ref.shape[1]
    earlier = (
        lax.broadcasted_iota(jnp.int32, (clen, clen), 0)
        < lax.broadcasted_iota(jnp.int32, (clen, clen), 1)
    ).astype(jnp.bfloat16)
    ones = jnp.ones((8, rr), jnp.bfloat16)
    target = lax.broadcasted_iota(jnp.int32, (padded, clen), 0)
    target = jnp.where(target < kept, target, 0)
    keeps = []
    for i in range(some):
        rows = rows_ref[pl.ds(ids_ref[pl.program_id(0) * some + i], 1), :]
        hit = (lax.broadcasted_iota(jnp.int32, (clen, rr), 0) == rows).astype(jnp.bfloat16)
        gone = lax.dot_general(
            ones, hit, (((1,), (1,)), ((), ())), preferred_element_type=jnp.float32
        )
        keeps.append(1.0 - gone)
    ranks = jnp.dot(
        jnp.concatenate(keeps, axis=0).astype(jnp.bfloat16),
        earlier,
        preferred_element_type=jnp.float32,
    )
    for i in range(some):
        rank = ranks[8 * i : 8 * i + 1].astype(jnp.int32)
        rank = jnp.where(keeps[i][:1] > 0.5, rank, -1)
        pick = (target == rank).astype(jnp.bfloat16)
        for layer in range(layers):
            both = jnp.concatenate([ck_ref[layer, i], cv_ref[layer, i]], axis=1)
            out_ref[layer, i] = jnp.dot(
                pick, both, preferred_element_type=jnp.float32
            ).astype(out_ref.dtype)


def compact(ids, recompute_rows, cache_keys, cache_values, kept, padded):
    layers, spans, clen, width = cache_keys.shape
    some = spans // 2
    cache_spec = pl.BlockSpec((layers, some, clen, width), lambda i, ids: (0, i, 0, 0))
    return pl.pallas_call(
        functools.partial(compact_kernel, kept=kept),
        grid_spec=pltpu.PrefetchScalarGridSpec(
            num_scalar_prefetch=1,
            grid=(spans // some,),
            in_specs=[
                pl.BlockSpec(recompute_rows.shape, lambda i, ids: (0, 0)),
                cache_spec,
                cache_spec,
            ],
            out_specs=pl.BlockSpec(
                (layers, some, padded, 2 * width), lambda i, ids: (0, i, 0, 0)
            ),
        ),
        out_shape=jax.ShapeDtypeStruct((layers, spans, padded, 2 * width), jnp.bfloat16),
        compiler_params=pltpu.CompilerParams(vmem_limit_bytes=56 * MIB),
        cost_estimate=pl.CostEstimate(
            flops=2 * layers * spans * padded * clen * 2 * width,
            bytes_accessed=8 * layers * spans * clen * width,
            transcendentals=0,
        ),
        name="compact",
    )(ids, recompute_rows, cache_keys, cache_values)


def spread_kernel(local_ref, packed_ref, main_ref, rest_ref, sem, *, groups, cut):
    layers, _, padded, _ = packed_ref.shape

    def copies(g):
        made = []
        for layer in range(layers):
            dest = layer * groups + g
            made.append(
                pltpu.make_async_copy(
                    packed_ref.at[layer, local_ref[g], pl.ds(0, cut)],
                    main_ref.at[dest],
                    sem.at[0, dest],
                )
            )
            made.append(
                pltpu.make_async_copy(
                    packed_ref.at[layer, local_ref[g], pl.ds(cut, padded - cut)],
                    rest_ref.at[dest],
                    sem.at[1, dest],
                )
            )
        return made

    for g in range(groups):

        @pl.when(local_ref[g] >= 0)
        def _():
            for copy in copies(g):
                copy.start()

    for g in range(groups):

        @pl.when(local_ref[g] >= 0)
        def _():
            for copy in copies(g):
                copy.wait()


def spread(local, packed, cut):
    layers, spans, padded, wide = packed.shape
    groups = local.shape[0]
    dests = layers * groups
    return pl.pallas_call(
        functools.partial(spread_kernel, groups=groups, cut=cut),
        in_specs=[
            pl.BlockSpec(memory_space=pltpu.SMEM),
            pl.BlockSpec(memory_space=pltpu.VMEM),
        ],
        out_specs=[pl.BlockSpec(memory_space=pl.ANY), pl.BlockSpec(memory_space=pl.ANY)],
        out_shape=[
            jax.ShapeDtypeStruct((dests, cut, wide), jnp.bfloat16),
            jax.ShapeDtypeStruct((dests, padded - cut, wide), jnp.bfloat16),
        ],
        scratch_shapes=[pltpu.SemaphoreType.DMA((2, dests))],
        compiler_params=pltpu.CompilerParams(vmem_limit_bytes=56 * MIB),
        cost_estimate=pl.CostEstimate(
            flops=0, bytes_accessed=2 * (dests + layers * spans) * padded * wide, transcendentals=0
        ),
        name="spread",
    )(local, packed)


def project_kernel(dest_ref, hidden_ref, wk_ref, wv_ref, *rest, rrows, slot):
    out_refs, rows_ref, result_ref = rest[:-2], rest[-2], rest[-1]
    _, reqs, topk, _, _ = hidden_ref.shape
    step = pl.program_id(0)

    @pl.when(step == 0)
    def _():
        for r in range(reqs):
            for j in range(topk):
                at = (r * topk + j) * slot
                rows_ref[at : at + rrows] = hidden_ref[0, r, j]
                if slot > rrows:
                    rows_ref[at + rrows : at + slot] = hidden_ref[0, r, j, : slot - rrows]

    weight = jnp.concatenate([wk_ref[0], wv_ref[0]], axis=1)
    result_ref[...] = jnp.dot(
        rows_ref[...], weight, preferred_element_type=jnp.float32
    ).astype(result_ref.dtype)
    for k, out_ref in enumerate(out_refs):

        @pl.when(step == k)
        def _():
            out_ref[...] = result_ref[...]


def project(dests, hidden, w_key, w_value, slot):
    _, reqs, topk, rrows, feats = hidden.shape
    spans = reqs * topk
    parts = dests.shape[0]
    share = w_key.shape[2] // parts
    shape = (spans * slot, 2 * share)
    return pl.pallas_call(
        functools.partial(project_kernel, rrows=rrows, slot=slot),
        grid_spec=pltpu.PrefetchScalarGridSpec(
            num_scalar_prefetch=1,
            grid=(parts,),
            in_specs=[
                pl.BlockSpec(hidden.shape, lambda p, to: (0, 0, 0, 0, 0)),
                pl.BlockSpec((1, feats, share), lambda p, to: (0, 0, to[p])),
                pl.BlockSpec((1, feats, share), lambda p, to: (0, 0, to[p])),
            ],
            out_specs=[pl.BlockSpec(shape, lambda p, to: (0, 0))] * parts,
            scratch_shapes=[
                pltpu.VMEM((spans * slot, feats), jnp.bfloat16),
                pltpu.VMEM(shape, jnp.bfloat16),
            ],
        ),
        out_shape=[jax.ShapeDtypeStruct(shape, jnp.bfloat16)] * parts,
        compiler_params=pltpu.CompilerParams(vmem_limit_bytes=56 * MIB),
        cost_estimate=pl.CostEstimate(
            flops=4 * parts * spans * slot * feats * share,
            bytes_accessed=2 * spans * rrows * feats + 4 * parts * (feats + spans * slot) * share,
            transcendentals=0,
        ),
        name="project",
    )(dests, hidden, w_key, w_value)


def attend_head(q, key_ref, wide_ref, state, causal):
    qlen = q.shape[0]
    count = key_ref.shape[0]
    factor = LOG2E / (HD ** 0.5)
    scores = lax.dot_general(
        q, key_ref[...], (((1,), (1,)), ((), ())), preferred_element_type=jnp.float32
    )
    if causal is not None:
        scores = jnp.concatenate(
            [scores[:, : count - qlen], jnp.where(causal, scores[:, count - qlen :], -1e30)],
            axis=1,
        )
    top = jnp.max(scores, axis=1, keepdims=True) * factor
    if state is not None:
        old = state[:, 2 * HD - 1 :]
        top = jnp.maximum(old, top)
    probs = jnp.exp2(scores * factor - top).astype(jnp.bfloat16)
    total = jnp.dot(probs, wide_ref[...], preferred_element_type=jnp.float32)
    if state is not None:
        total = total + state * jnp.exp2(old - top)
    return total, top


def pack_state(total, top):
    lane = lax.broadcasted_iota(jnp.int32, total.shape, 1)
    return jnp.where(lane < 2 * HD - HD // 2, total, top)


def gather_keys(blocks, key_ref, wide_ref, kept):
    rows = blocks[0].shape[1]
    real = lax.broadcasted_iota(jnp.int32, (rows, HD), 0) < kept
    for j, ref in enumerate(blocks):
        span = slice(j * rows, (j + 1) * rows)
        key_ref[span] = ref[0, :, :HD]
        value = ref[0, :, HD:]
        if kept < rows:
            value = jnp.where(real, value, 0).astype(jnp.bfloat16)
        wide_ref[span, :HD] = value
        wide_ref[span, HD:] = real.astype(jnp.bfloat16)


def own_kernel(q_ref, nk_ref, nv_ref, *rest, rrows, slot):
    out_ref, key_ref, wide_ref = rest[-3:]
    pieces = rest[:-3]
    fresh_rows = pieces[0].shape[0]
    qlen = nk_ref.shape[2]

    @pl.when(pl.program_id(1) == 0)
    def _():
        real = lax.broadcasted_iota(jnp.int32, (fresh_rows, HD), 0) % slot < rrows
        fresh = pieces[0][...].astype(jnp.float32)
        for piece in pieces[1:]:
            fresh = fresh + piece[...].astype(jnp.float32)
        key_ref[:fresh_rows] = fresh[:, :HD].astype(jnp.bfloat16)
        wide_ref[:fresh_rows, :HD] = jnp.where(real, fresh[:, HD:], 0).astype(jnp.bfloat16)
        wide_ref[:fresh_rows, HD:] = real.astype(jnp.bfloat16)
        key_ref[fresh_rows:] = nk_ref[0, 0]
        wide_ref[fresh_rows:, :HD] = nv_ref[0, 0]
        wide_ref[fresh_rows:, HD:] = jnp.ones((qlen, HD), jnp.bfloat16)

    causal = lax.broadcasted_iota(jnp.int32, (qlen, qlen), 0) >= lax.broadcasted_iota(
        jnp.int32, (qlen, qlen), 1
    )
    for h in range(out_ref.shape[1]):
        q = q_ref[0, 0, :, h * HD : (h + 1) * HD]
        out_ref[0, h] = pack_state(*attend_head(q, key_ref, wide_ref, None, causal))


def main_kernel(place_ref, q_ref, state_ref, *rest):
    out_ref, key_ref, wide_ref = rest[-3:]
    blocks = rest[:-3]

    @pl.when(pl.program_id(1) == 0)
    def _():
        gather_keys(blocks, key_ref, wide_ref, blocks[0].shape[1])

    for h in range(out_ref.shape[1]):
        q = q_ref[0, 0, :, h * HD : (h + 1) * HD]
        out_ref[0, h] = pack_state(*attend_head(q, key_ref, wide_ref, state_ref[0, h], None))


def last_kernel(place_ref, q_ref, state_ref, *rest, kept):
    out_ref, key_ref, wide_ref = rest[-3:]
    blocks = rest[:-3]

    @pl.when(pl.program_id(1) == 0)
    def _():
        gather_keys(blocks, key_ref, wide_ref, kept)

    for h in range(state_ref.shape[1]):
        lanes = slice(h * HD, (h + 1) * HD)
        total, _ = attend_head(
            q_ref[0, 0, :, lanes], key_ref, wide_ref, state_ref[0, h], None
        )
        out_ref[0, 0, :, lanes] = (total[:, :HD] / total[:, HD : HD + 1]).astype(out_ref.dtype)


def attend_cost(reqs, heads, qlen, count):
    return pl.CostEstimate(
        flops=6 * reqs * heads * qlen * count * HD,
        bytes_accessed=4 * reqs * count * HD + 16 * reqs * heads * qlen * HD,
        transcendentals=reqs * heads * qlen * count,
    )


def attend_own(queries, pieces, query_keys, query_values, rrows, slot):
    _, reqs, qlen, feats = queries.shape
    heads = feats // HD
    some = heads // 2
    fresh_rows = pieces[0].shape[0] // reqs
    count = fresh_rows + qlen
    return pl.pallas_call(
        functools.partial(own_kernel, rrows=rrows, slot=slot),
        grid=(reqs, heads // some),
        in_specs=[
            pl.BlockSpec((1, 1, qlen, some * HD), lambda r, h: (0, r, 0, h)),
            pl.BlockSpec((1, 1, qlen, HD), lambda r, h: (0, r, 0, 0)),
            pl.BlockSpec((1, 1, qlen, HD), lambda r, h: (0, r, 0, 0)),
        ]
        + [pl.BlockSpec((fresh_rows, 2 * HD), lambda r, h: (r, 0))] * len(pieces),
        out_specs=pl.BlockSpec((1, some, qlen, 2 * HD), lambda r, h: (r, h, 0, 0)),
        out_shape=jax.ShapeDtypeStruct((reqs, heads, qlen, 2 * HD), jnp.float32),
        scratch_shapes=[
            pltpu.VMEM((count, HD), jnp.bfloat16),
            pltpu.VMEM((count, 2 * HD), jnp.bfloat16),
        ],
        compiler_params=pltpu.CompilerParams(vmem_limit_bytes=56 * MIB),
        cost_estimate=attend_cost(reqs, heads, qlen, count),
        name="attend_own",
    )(queries, query_keys, query_values, *pieces)


def attend_spans(place, queries, state, arrived, kept, last):
    _, reqs, qlen, feats = queries.shape
    heads = feats // HD
    some = heads
    rows = arrived.shape[1]
    topk = place.shape[0] // reqs
    count = topk * rows
    q_spec = pl.BlockSpec((1, 1, qlen, some * HD), lambda r, h, at: (0, r, 0, h))
    state_spec = pl.BlockSpec((1, some, qlen, 2 * HD), lambda r, h, at: (r, h, 0, 0))
    blocks = [
        pl.BlockSpec((1, rows, 2 * HD), lambda r, h, at, j=j: (at[r * topk + j], 0, 0))
        for j in range(topk)
    ]
    return pl.pallas_call(
        functools.partial(last_kernel, kept=kept) if last else main_kernel,
        grid_spec=pltpu.PrefetchScalarGridSpec(
            num_scalar_prefetch=1,
            grid=(reqs, heads // some),
            in_specs=[q_spec, state_spec] + blocks,
            out_specs=q_spec if last else state_spec,
            scratch_shapes=[
                pltpu.VMEM((count, HD), jnp.bfloat16),
                pltpu.VMEM((count, 2 * HD), jnp.bfloat16),
            ],
        ),
        out_shape=jax.ShapeDtypeStruct(queries.shape, jnp.bfloat16)
        if last
        else jax.ShapeDtypeStruct(state.shape, state.dtype),
        compiler_params=pltpu.CompilerParams(vmem_limit_bytes=56 * MIB),
        cost_estimate=attend_cost(reqs, heads, qlen, count),
        name="attend_last" if last else "attend_main",
    )(place, queries, state, *([arrived] * topk))


def on_device(
    cache_keys,
    cache_values,
    span_ids,
    owner_slot,
    recompute_rows,
    hidden,
    w_key,
    w_value,
    queries,
    query_keys,
    query_values,
):
    sections = lax.axis_size("section")
    groups = lax.axis_size("dp")
    parts = lax.axis_size("tensor")
    per_owner = cache_keys.shape[1]
    clen = cache_keys.shape[2]
    req_dev, topk = span_ids.shape
    rrows = hidden.shape[3]
    kept = clen - rrows
    cut = kept // HD * HD
    padded = ceil_to(kept, 64)
    slot = ceil_to(rrows, TILE)
    myself = lax.axis_index("section") * groups + lax.axis_index("dp")

    own_slot = owner_slot[span_ids].reshape(req_dev * topk)
    every_slot = lax.all_to_all(
        jnp.broadcast_to(own_slot[None], (groups, req_dev * topk)), "dp", 0, 0
    )

    here = myself * per_owner + jnp.arange(per_owner, dtype=jnp.int32)
    held = owner_slot[None, :] == here[:, None]
    ids = jnp.sum(
        jnp.where(held, jnp.arange(owner_slot.shape[0], dtype=jnp.int32)[None], 0), axis=1
    )
    packed = compact(ids, recompute_rows, cache_keys, cache_values, kept, padded)

    mine = every_slot // per_owner == myself
    local = jnp.max(jnp.where(mine, every_slot % per_owner, -1), axis=1)
    main, rest = spread(local, packed, cut)
    main, hidden = lax.optimization_barrier((main, hidden))
    moves = [(i // 2, i % 2) for i in range(parts)]

    def moved(index, move):
        return (index // 2 + move[0]) % (parts // 2) * 2 + (index + move[1]) % 2

    me = lax.axis_index("tensor")
    dests = jnp.stack([moved(me, move) for move in moves]).astype(jnp.int32)
    partial = project(dests, hidden, w_key, w_value, slot)
    arrived = lax.all_to_all(main, ("section", "dp"), 0, 0, tiled=True)
    pieces = [partial[0]] + [
        lax.ppermute(piece, "tensor", [(i, moved(i, move)) for i in range(parts)])
        for piece, move in zip(partial[1:], moves[1:])
    ]
    state = attend_own(queries, pieces, query_keys, query_values, rrows, slot)
    rest, arrived, state = lax.optimization_barrier((rest, arrived, state))
    arrived_rest = lax.all_to_all(rest, ("section", "dp"), 0, 0, tiled=True)

    place = own_slot // per_owner
    state = attend_spans(place, queries, state, arrived, cut, False)
    return attend_spans(place, queries, state, arrived_rest, kept - cut, True)


def solution(mesh):
    in_specs = (
        P(None, ("section", "dp"), None, "tensor"),
        P(None, ("section", "dp"), None, "tensor"),
        P("dp", None),
        P(),
        P(),
        P("section", "dp", None, None, "tensor"),
        P("section", "tensor", None),
        P("section", "tensor", None),
        P("section", "dp", None, "tensor"),
        P("section", "dp", None, "tensor"),
        P("section", "dp", None, "tensor"),
    )
    out_specs = P("section", "dp", None, "tensor")
    return jax.shard_map(
        on_device, mesh=mesh, in_specs=in_specs, out_specs=out_specs, check_vma=False
    )
```

```python
import functools

import jax
import jax.numpy as jnp
from jax import lax
from jax.experimental import pallas as pl
from jax.experimental.pallas import tpu as pltpu
from jax.sharding import PartitionSpec as P

HD = 128
TILE = 16
MIB = 1 << 20
LOG2E = 1.4426950408889634


def ceil_to(n, m):
    return -(-n // m) * m


def compact_kernel(ids_ref, rows_ref, ck_ref, cv_ref, out_ref, *, kept):
    layers, some, clen, width = ck_ref.shape
    padded = out_ref.shape[2]
    rr = rows_ref.shape[1]
    earlier = (
        lax.broadcasted_iota(jnp.int32, (clen, clen), 0)
        < lax.broadcasted_iota(jnp.int32, (clen, clen), 1)
    ).astype(jnp.bfloat16)
    ones = jnp.ones((8, rr), jnp.bfloat16)
    target = lax.broadcasted_iota(jnp.int32, (padded, clen), 0)
    target = jnp.where(target < kept, target, 0)
    keeps = []
    for i in range(some):
        rows = rows_ref[pl.ds(ids_ref[pl.program_id(0) * some + i], 1), :]
        hit = (lax.broadcasted_iota(jnp.int32, (clen, rr), 0) == rows).astype(jnp.bfloat16)
        gone = lax.dot_general(
            ones, hit, (((1,), (1,)), ((), ())), preferred_element_type=jnp.float32
        )
        keeps.append(1.0 - gone)
    ranks = jnp.dot(
        jnp.concatenate(keeps, axis=0).astype(jnp.bfloat16),
        earlier,
        preferred_element_type=jnp.float32,
    )
    for i in range(some):
        rank = ranks[8 * i : 8 * i + 1].astype(jnp.int32)
        rank = jnp.where(keeps[i][:1] > 0.5, rank, -1)
        pick = (target == rank).astype(jnp.bfloat16)
        for layer in range(layers):
            both = jnp.concatenate([ck_ref[layer, i], cv_ref[layer, i]], axis=1)
            out_ref[layer, i] = jnp.dot(
                pick, both, preferred_element_type=jnp.float32
            ).astype(out_ref.dtype)


def compact(ids, recompute_rows, cache_keys, cache_values, kept, padded):
    layers, spans, clen, width = cache_keys.shape
    some = spans // 2
    cache_spec = pl.BlockSpec((layers, some, clen, width), lambda i, ids: (0, i, 0, 0))
    return pl.pallas_call(
        functools.partial(compact_kernel, kept=kept),
        grid_spec=pltpu.PrefetchScalarGridSpec(
            num_scalar_prefetch=1,
            grid=(spans // some,),
            in_specs=[
                pl.BlockSpec(recompute_rows.shape, lambda i, ids: (0, 0)),
                cache_spec,
                cache_spec,
            ],
            out_specs=pl.BlockSpec(
                (layers, some, padded, 2 * width), lambda i, ids: (0, i, 0, 0)
            ),
        ),
        out_shape=jax.ShapeDtypeStruct((layers, spans, padded, 2 * width), jnp.bfloat16),
        compiler_params=pltpu.CompilerParams(vmem_limit_bytes=56 * MIB),
        cost_estimate=pl.CostEstimate(
            flops=2 * layers * spans * padded * clen * 2 * width,
            bytes_accessed=8 * layers * spans * clen * width,
            transcendentals=0,
        ),
        name="compact",
    )(ids, recompute_rows, cache_keys, cache_values)


def spread_kernel(local_ref, packed_ref, main_ref, rest_ref, sem, *, groups, cut):
    layers, _, padded, _ = packed_ref.shape

    def copies(g):
        made = []
        for layer in range(layers):
            dest = layer * groups + g
            made.append(
                pltpu.make_async_copy(
                    packed_ref.at[layer, local_ref[g], pl.ds(0, cut)],
                    main_ref.at[dest],
                    sem.at[0, dest],
                )
            )
            made.append(
                pltpu.make_async_copy(
                    packed_ref.at[layer, local_ref[g], pl.ds(cut, padded - cut)],
                    rest_ref.at[dest],
                    sem.at[1, dest],
                )
            )
        return made

    for g in range(groups):

        @pl.when(local_ref[g] >= 0)
        def _():
            for copy in copies(g):
                copy.start()

    for g in range(groups):

        @pl.when(local_ref[g] >= 0)
        def _():
            for copy in copies(g):
                copy.wait()


def spread(local, packed, cut):
    layers, spans, padded, wide = packed.shape
    groups = local.shape[0]
    dests = layers * groups
    return pl.pallas_call(
        functools.partial(spread_kernel, groups=groups, cut=cut),
        in_specs=[
            pl.BlockSpec(memory_space=pltpu.SMEM),
            pl.BlockSpec(memory_space=pltpu.VMEM),
        ],
        out_specs=[pl.BlockSpec(memory_space=pl.ANY), pl.BlockSpec(memory_space=pl.ANY)],
        out_shape=[
            jax.ShapeDtypeStruct((dests, cut, wide), jnp.bfloat16),
            jax.ShapeDtypeStruct((dests, padded - cut, wide), jnp.bfloat16),
        ],
        scratch_shapes=[pltpu.SemaphoreType.DMA((2, dests))],
        compiler_params=pltpu.CompilerParams(vmem_limit_bytes=56 * MIB),
        cost_estimate=pl.CostEstimate(
            flops=0, bytes_accessed=2 * (dests + layers * spans) * padded * wide, transcendentals=0
        ),
        name="spread",
    )(local, packed)


def project_kernel(dest_ref, hidden_ref, wk_ref, wv_ref, *rest, rrows, slot):
    out_refs, rows_ref, result_ref = rest[:-2], rest[-2], rest[-1]
    _, reqs, topk, _, _ = hidden_ref.shape
    step = pl.program_id(0)

    @pl.when(step == 0)
    def _():
        for r in range(reqs):
            for j in range(topk):
                at = (r * topk + j) * slot
                rows_ref[at : at + rrows] = hidden_ref[0, r, j]
                if slot > rrows:
                    rows_ref[at + rrows : at + slot] = hidden_ref[0, r, j, : slot - rrows]

    weight = jnp.concatenate([wk_ref[0], wv_ref[0]], axis=1)
    result_ref[...] = jnp.dot(
        rows_ref[...], weight, preferred_element_type=jnp.float32
    ).astype(result_ref.dtype)
    count = result_ref.shape[0]
    for k, out_ref in enumerate(out_refs):
        for half in range(2):

            @pl.when(step == 2 * k + half)
            def _():
                out_ref[half * count : (half + 1) * count] = result_ref[...]


def project(dests, hidden, w_key, w_value, slot):
    _, reqs, topk, rrows, feats = hidden.shape
    spans = reqs * topk
    parts = dests.shape[0]
    share = w_key.shape[2] // parts
    shape = (spans * slot, 2 * share)
    pair = (2 * spans * slot, 2 * share)
    return pl.pallas_call(
        functools.partial(project_kernel, rrows=rrows, slot=slot),
        grid_spec=pltpu.PrefetchScalarGridSpec(
            num_scalar_prefetch=1,
            grid=(parts,),
            in_specs=[
                pl.BlockSpec(hidden.shape, lambda p, to: (0, 0, 0, 0, 0)),
                pl.BlockSpec((1, feats, share), lambda p, to: (0, 0, to[p])),
                pl.BlockSpec((1, feats, share), lambda p, to: (0, 0, to[p])),
            ],
            out_specs=[pl.BlockSpec(pair, lambda p, to: (0, 0))] * (parts // 2),
            scratch_shapes=[
                pltpu.VMEM((spans * slot, feats), jnp.bfloat16),
                pltpu.VMEM(shape, jnp.bfloat16),
            ],
        ),
        out_shape=[jax.ShapeDtypeStruct(pair, jnp.bfloat16)] * (parts // 2),
        compiler_params=pltpu.CompilerParams(vmem_limit_bytes=56 * MIB),
        cost_estimate=pl.CostEstimate(
            flops=4 * parts * spans * slot * feats * share,
            bytes_accessed=2 * spans * rrows * feats + 4 * parts * (feats + spans * slot) * share,
            transcendentals=0,
        ),
        name="project",
    )(dests, hidden, w_key, w_value)


def attend_head(q, key_ref, wide_ref, state, causal):
    qlen = q.shape[0]
    count = key_ref.shape[0]
    factor = LOG2E / (HD ** 0.5)
    scores = lax.dot_general(
        q, key_ref[...], (((1,), (1,)), ((), ())), preferred_element_type=jnp.float32
    )
    if causal is not None:
        scores = jnp.concatenate(
            [scores[:, : count - qlen], jnp.where(causal, scores[:, count - qlen :], -1e30)],
            axis=1,
        )
    top = jnp.max(scores, axis=1, keepdims=True) * factor
    if state is not None:
        old = state[:, 2 * HD - 1 :]
        top = jnp.maximum(old, top)
    probs = jnp.exp2(scores * factor - top).astype(jnp.bfloat16)
    total = jnp.dot(probs, wide_ref[...], preferred_element_type=jnp.float32)
    if state is not None:
        total = total + state * jnp.exp2(old - top)
    return total, top


def pack_state(total, top):
    lane = lax.broadcasted_iota(jnp.int32, total.shape, 1)
    return jnp.where(lane < 2 * HD - HD // 2, total, top)


def gather_keys(blocks, key_ref, wide_ref, kept):
    rows = blocks[0].shape[1]
    real = lax.broadcasted_iota(jnp.int32, (rows, HD), 0) < kept
    for j, ref in enumerate(blocks):
        span = slice(j * rows, (j + 1) * rows)
        key_ref[span] = ref[0, :, :HD]
        value = ref[0, :, HD:]
        if kept < rows:
            value = jnp.where(real, value, 0).astype(jnp.bfloat16)
        wide_ref[span, :HD] = value
        wide_ref[span, HD:] = real.astype(jnp.bfloat16)


def own_kernel(q_ref, nk_ref, nv_ref, *rest, rrows, slot):
    out_ref, key_ref, wide_ref = rest[-3:]
    pieces = rest[:-3]
    fresh_rows = pieces[0].shape[0]
    qlen = nk_ref.shape[2]

    @pl.when(pl.program_id(1) == 0)
    def _():
        real = lax.broadcasted_iota(jnp.int32, (fresh_rows, HD), 0) % slot < rrows
        fresh = pieces[0][...].astype(jnp.float32)
        for piece in pieces[1:]:
            fresh = fresh + piece[...].astype(jnp.float32)
        key_ref[:fresh_rows] = fresh[:, :HD].astype(jnp.bfloat16)
        wide_ref[:fresh_rows, :HD] = jnp.where(real, fresh[:, HD:], 0).astype(jnp.bfloat16)
        wide_ref[:fresh_rows, HD:] = real.astype(jnp.bfloat16)
        key_ref[fresh_rows:] = nk_ref[0, 0]
        wide_ref[fresh_rows:, :HD] = nv_ref[0, 0]
        wide_ref[fresh_rows:, HD:] = jnp.ones((qlen, HD), jnp.bfloat16)

    causal = lax.broadcasted_iota(jnp.int32, (qlen, qlen), 0) >= lax.broadcasted_iota(
        jnp.int32, (qlen, qlen), 1
    )
    for h in range(out_ref.shape[1]):
        q = q_ref[0, 0, :, h * HD : (h + 1) * HD]
        out_ref[0, h] = pack_state(*attend_head(q, key_ref, wide_ref, None, causal))


def main_kernel(place_ref, q_ref, state_ref, *rest):
    out_ref, key_ref, wide_ref = rest[-3:]
    blocks = rest[:-3]

    @pl.when(pl.program_id(1) == 0)
    def _():
        gather_keys(blocks, key_ref, wide_ref, blocks[0].shape[1])

    for h in range(out_ref.shape[1]):
        q = q_ref[0, 0, :, h * HD : (h + 1) * HD]
        out_ref[0, h] = pack_state(*attend_head(q, key_ref, wide_ref, state_ref[0, h], None))


def last_kernel(place_ref, q_ref, state_ref, *rest, kept):
    out_ref, key_ref, wide_ref = rest[-3:]
    blocks = rest[:-3]

    @pl.when(pl.program_id(1) == 0)
    def _():
        gather_keys(blocks, key_ref, wide_ref, kept)

    for h in range(state_ref.shape[1]):
        lanes = slice(h * HD, (h + 1) * HD)
        total, _ = attend_head(
            q_ref[0, 0, :, lanes], key_ref, wide_ref, state_ref[0, h], None
        )
        out_ref[0, 0, :, lanes] = (total[:, :HD] / total[:, HD : HD + 1]).astype(out_ref.dtype)


def attend_cost(reqs, heads, qlen, count):
    return pl.CostEstimate(
        flops=6 * reqs * heads * qlen * count * HD,
        bytes_accessed=4 * reqs * count * HD + 16 * reqs * heads * qlen * HD,
        transcendentals=reqs * heads * qlen * count,
    )


def attend_own(queries, pieces, query_keys, query_values, rrows, slot):
    _, reqs, qlen, feats = queries.shape
    heads = feats // HD
    some = heads // 2
    fresh_rows = pieces[-1].shape[0] // reqs
    count = fresh_rows + qlen
    return pl.pallas_call(
        functools.partial(own_kernel, rrows=rrows, slot=slot),
        grid=(reqs, heads // some),
        in_specs=[
            pl.BlockSpec((1, 1, qlen, some * HD), lambda r, h: (0, r, 0, h)),
            pl.BlockSpec((1, 1, qlen, HD), lambda r, h: (0, r, 0, 0)),
            pl.BlockSpec((1, 1, qlen, HD), lambda r, h: (0, r, 0, 0)),
        ]
        + [pl.BlockSpec((fresh_rows, 2 * HD), lambda r, h: (r, 0))] * len(pieces),
        out_specs=pl.BlockSpec((1, some, qlen, 2 * HD), lambda r, h: (r, h, 0, 0)),
        out_shape=jax.ShapeDtypeStruct((reqs, heads, qlen, 2 * HD), jnp.float32),
        scratch_shapes=[
            pltpu.VMEM((count, HD), jnp.bfloat16),
            pltpu.VMEM((count, 2 * HD), jnp.bfloat16),
        ],
        compiler_params=pltpu.CompilerParams(vmem_limit_bytes=56 * MIB),
        cost_estimate=attend_cost(reqs, heads, qlen, count),
        name="attend_own",
    )(queries, query_keys, query_values, *pieces)


def attend_spans(place, queries, state, arrived, kept, last):
    _, reqs, qlen, feats = queries.shape
    heads = feats // HD
    some = heads
    rows = arrived.shape[1]
    topk = place.shape[0] // reqs
    count = topk * rows
    q_spec = pl.BlockSpec((1, 1, qlen, some * HD), lambda r, h, at: (0, r, 0, h))
    state_spec = pl.BlockSpec((1, some, qlen, 2 * HD), lambda r, h, at: (r, h, 0, 0))
    blocks = [
        pl.BlockSpec((1, rows, 2 * HD), lambda r, h, at, j=j: (at[r * topk + j], 0, 0))
        for j in range(topk)
    ]
    return pl.pallas_call(
        functools.partial(last_kernel, kept=kept) if last else main_kernel,
        grid_spec=pltpu.PrefetchScalarGridSpec(
            num_scalar_prefetch=1,
            grid=(reqs, heads // some),
            in_specs=[q_spec, state_spec] + blocks,
            out_specs=q_spec if last else state_spec,
            scratch_shapes=[
                pltpu.VMEM((count, HD), jnp.bfloat16),
                pltpu.VMEM((count, 2 * HD), jnp.bfloat16),
            ],
        ),
        out_shape=jax.ShapeDtypeStruct(queries.shape, jnp.bfloat16)
        if last
        else jax.ShapeDtypeStruct(state.shape, state.dtype),
        compiler_params=pltpu.CompilerParams(vmem_limit_bytes=56 * MIB),
        cost_estimate=attend_cost(reqs, heads, qlen, count),
        name="attend_last" if last else "attend_main",
    )(place, queries, state, *([arrived] * topk))


def on_device(
    cache_keys,
    cache_values,
    span_ids,
    owner_slot,
    recompute_rows,
    hidden,
    w_key,
    w_value,
    queries,
    query_keys,
    query_values,
):
    sections = lax.axis_size("section")
    groups = lax.axis_size("dp")
    parts = lax.axis_size("tensor")
    per_owner = cache_keys.shape[1]
    clen = cache_keys.shape[2]
    req_dev, topk = span_ids.shape
    rrows = hidden.shape[3]
    kept = clen - rrows
    cut = kept // HD * HD
    padded = ceil_to(kept, 64)
    slot = ceil_to(rrows, TILE)
    myself = lax.axis_index("section") * groups + lax.axis_index("dp")

    own_slot = owner_slot[span_ids].reshape(req_dev * topk)
    every_slot = lax.all_to_all(
        jnp.broadcast_to(own_slot[None], (groups, req_dev * topk)), "dp", 0, 0
    )

    here = myself * per_owner + jnp.arange(per_owner, dtype=jnp.int32)
    held = owner_slot[None, :] == here[:, None]
    ids = jnp.sum(
        jnp.where(held, jnp.arange(owner_slot.shape[0], dtype=jnp.int32)[None], 0), axis=1
    )
    packed = compact(ids, recompute_rows, cache_keys, cache_values, kept, padded)

    mine = every_slot // per_owner == myself
    local = jnp.max(jnp.where(mine, every_slot % per_owner, -1), axis=1)
    main, rest = spread(local, packed, cut)
    main, hidden = lax.optimization_barrier((main, hidden))
    moves = [(i // 2, i % 2) for i in range(parts)]

    def moved(index, move):
        return (index // 2 + move[0]) % (parts // 2) * 2 + (index + move[1]) % 2

    me = lax.axis_index("tensor")
    dests = jnp.stack([moved(me, move) for move in moves]).astype(jnp.int32)
    partial = project(dests, hidden, w_key, w_value, slot)
    arrived = lax.all_to_all(main, ("section", "dp"), 0, 0, tiled=True)
    pieces = [partial[0]] + [
        lax.ppermute(piece, "tensor", [(i, moved(i, (shift, 0))) for i in range(parts)])
        for shift, piece in enumerate(partial[1:], 1)
    ]
    count = req_dev * topk * slot
    across = sum(piece[count:].astype(jnp.float32) for piece in pieces).astype(jnp.bfloat16)
    pieces.append(
        lax.ppermute(across, "tensor", [(i, moved(i, (0, 1))) for i in range(parts)])
    )
    state = attend_own(queries, pieces, query_keys, query_values, rrows, slot)
    rest, arrived, state = lax.optimization_barrier((rest, arrived, state))
    arrived_rest = lax.all_to_all(rest, ("section", "dp"), 0, 0, tiled=True)

    place = own_slot // per_owner
    state = attend_spans(place, queries, state, arrived, cut, False)
    return attend_spans(place, queries, state, arrived_rest, kept - cut, True)


def solution(mesh):
    in_specs = (
        P(None, ("section", "dp"), None, "tensor"),
        P(None, ("section", "dp"), None, "tensor"),
        P("dp", None),
        P(),
        P(),
        P("section", "dp", None, None, "tensor"),
        P("section", "tensor", None),
        P("section", "tensor", None),
        P("section", "dp", None, "tensor"),
        P("section", "dp", None, "tensor"),
        P("section", "dp", None, "tensor"),
    )
    out_specs = P("section", "dp", None, "tensor")
    return jax.shard_map(
        on_device, mesh=mesh, in_specs=in_specs, out_specs=out_specs, check_vma=False
    )
```

```python
import functools

import jax
import jax.numpy as jnp
from jax import lax
from jax.experimental import pallas as pl
from jax.experimental.pallas import tpu as pltpu
from jax.sharding import PartitionSpec as P

HD = 128
TILE = 16
MIB = 1 << 20
LOG2E = 1.4426950408889634


def ceil_to(n, m):
    return -(-n // m) * m


def compact_kernel(ids_ref, rows_ref, ck_ref, cv_ref, out_ref, *, kept):
    layers, some, clen, width = ck_ref.shape
    padded = out_ref.shape[2]
    rr, all_spans = rows_ref.shape
    earlier = (
        lax.broadcasted_iota(jnp.int32, (clen, clen), 0)
        < lax.broadcasted_iota(jnp.int32, (clen, clen), 1)
    ).astype(jnp.bfloat16)
    ones = jnp.ones((8, rr), jnp.bfloat16)
    target = lax.broadcasted_iota(jnp.int32, (padded, clen), 0)
    target = jnp.where(target < kept, target, 0)
    keeps = []
    for i in range(some):
        span = ids_ref[pl.program_id(0) * some + i]
        this = lax.broadcasted_iota(jnp.int32, (rr, all_spans), 1) == span
        rows = jnp.sum(jnp.where(this, rows_ref[...], 0), axis=1, keepdims=True)
        hit = (lax.broadcasted_iota(jnp.int32, (rr, clen), 1) == rows).astype(jnp.bfloat16)
        gone = jnp.dot(ones, hit, preferred_element_type=jnp.float32)
        keeps.append(1.0 - gone)
    ranks = jnp.dot(
        jnp.concatenate(keeps, axis=0).astype(jnp.bfloat16),
        earlier,
        preferred_element_type=jnp.float32,
    )
    for i in range(some):
        rank = ranks[8 * i : 8 * i + 1].astype(jnp.int32)
        rank = jnp.where(keeps[i][:1] > 0.5, rank, -1)
        pick = (target == rank).astype(jnp.bfloat16)
        for layer in range(layers):
            both = jnp.concatenate([ck_ref[layer, i], cv_ref[layer, i]], axis=1)
            out_ref[layer, i] = jnp.dot(
                pick, both, preferred_element_type=jnp.float32
            ).astype(out_ref.dtype)


def compact(ids, recompute_rows, cache_keys, cache_values, kept, padded):
    layers, spans, clen, width = cache_keys.shape
    some = spans // 2
    cache_spec = pl.BlockSpec((layers, some, clen, width), lambda i, ids: (0, i, 0, 0))
    return pl.pallas_call(
        functools.partial(compact_kernel, kept=kept),
        grid_spec=pltpu.PrefetchScalarGridSpec(
            num_scalar_prefetch=1,
            grid=(spans // some,),
            in_specs=[
                pl.BlockSpec(recompute_rows.shape, lambda i, ids: (0, 0)),
                cache_spec,
                cache_spec,
            ],
            out_specs=pl.BlockSpec(
                (layers, some, padded, 2 * width), lambda i, ids: (0, i, 0, 0)
            ),
        ),
        out_shape=jax.ShapeDtypeStruct((layers, spans, padded, 2 * width), jnp.bfloat16),
        compiler_params=pltpu.CompilerParams(vmem_limit_bytes=56 * MIB),
        cost_estimate=pl.CostEstimate(
            flops=2 * layers * spans * padded * clen * 2 * width,
            bytes_accessed=8 * layers * spans * clen * width,
            transcendentals=0,
        ),
        name="compact",
    )(ids, recompute_rows, cache_keys, cache_values)


def spread_kernel(local_ref, packed_ref, main_ref, rest_ref, sem, *, groups, cut):
    layers, _, padded, _ = packed_ref.shape

    def copies(g):
        made = []
        for layer in range(layers):
            dest = layer * groups + g
            made.append(
                pltpu.make_async_copy(
                    packed_ref.at[layer, local_ref[g], pl.ds(0, cut)],
                    main_ref.at[dest],
                    sem.at[0, dest],
                )
            )
            made.append(
                pltpu.make_async_copy(
                    packed_ref.at[layer, local_ref[g], pl.ds(cut, padded - cut)],
                    rest_ref.at[dest],
                    sem.at[1, dest],
                )
            )
        return made

    for g in range(groups):

        @pl.when(local_ref[g] >= 0)
        def _():
            for copy in copies(g):
                copy.start()

    for g in range(groups):

        @pl.when(local_ref[g] >= 0)
        def _():
            for copy in copies(g):
                copy.wait()


def spread(local, packed, cut):
    layers, spans, padded, wide = packed.shape
    groups = local.shape[0]
    dests = layers * groups
    return pl.pallas_call(
        functools.partial(spread_kernel, groups=groups, cut=cut),
        in_specs=[
            pl.BlockSpec(memory_space=pltpu.SMEM),
            pl.BlockSpec(memory_space=pltpu.VMEM),
        ],
        out_specs=[pl.BlockSpec(memory_space=pl.ANY), pl.BlockSpec(memory_space=pl.ANY)],
        out_shape=[
            jax.ShapeDtypeStruct((dests, cut, wide), jnp.bfloat16),
            jax.ShapeDtypeStruct((dests, padded - cut, wide), jnp.bfloat16),
        ],
        scratch_shapes=[pltpu.SemaphoreType.DMA((2, dests))],
        compiler_params=pltpu.CompilerParams(vmem_limit_bytes=56 * MIB),
        cost_estimate=pl.CostEstimate(
            flops=0, bytes_accessed=2 * (dests + layers * spans) * padded * wide, transcendentals=0
        ),
        name="spread",
    )(local, packed)


def project_kernel(dest_ref, hidden_ref, wk_ref, wv_ref, *rest, rrows, slot):
    out_refs, rows_ref, result_ref = rest[:-2], rest[-2], rest[-1]
    _, reqs, topk, _, _ = hidden_ref.shape
    step = pl.program_id(0)

    @pl.when(step == 0)
    def _():
        for r in range(reqs):
            for j in range(topk):
                at = (r * topk + j) * slot
                rows_ref[at : at + rrows] = hidden_ref[0, r, j]
                if slot > rrows:
                    rows_ref[at + rrows : at + slot] = hidden_ref[0, r, j, : slot - rrows]

    weight = jnp.concatenate([wk_ref[0], wv_ref[0]], axis=1)
    result_ref[...] = jnp.dot(
        rows_ref[...], weight, preferred_element_type=jnp.float32
    ).astype(result_ref.dtype)
    count = result_ref.shape[0]
    for k, out_ref in enumerate(out_refs):
        for half in range(2):

            @pl.when(step == 2 * k + half)
            def _():
                out_ref[half * count : (half + 1) * count] = result_ref[...]


def project(dests, hidden, w_key, w_value, slot):
    _, reqs, topk, rrows, feats = hidden.shape
    spans = reqs * topk
    parts = dests.shape[0]
    share = w_key.shape[2] // parts
    shape = (spans * slot, 2 * share)
    pair = (2 * spans * slot, 2 * share)
    return pl.pallas_call(
        functools.partial(project_kernel, rrows=rrows, slot=slot),
        grid_spec=pltpu.PrefetchScalarGridSpec(
            num_scalar_prefetch=1,
            grid=(parts,),
            in_specs=[
                pl.BlockSpec(hidden.shape, lambda p, to: (0, 0, 0, 0, 0)),
                pl.BlockSpec((1, feats, share), lambda p, to: (0, 0, to[p])),
                pl.BlockSpec((1, feats, share), lambda p, to: (0, 0, to[p])),
            ],
            out_specs=[pl.BlockSpec(pair, lambda p, to: (0, 0))] * (parts // 2),
            scratch_shapes=[
                pltpu.VMEM((spans * slot, feats), jnp.bfloat16),
                pltpu.VMEM(shape, jnp.bfloat16),
            ],
        ),
        out_shape=[jax.ShapeDtypeStruct(pair, jnp.bfloat16)] * (parts // 2),
        compiler_params=pltpu.CompilerParams(vmem_limit_bytes=56 * MIB),
        cost_estimate=pl.CostEstimate(
            flops=4 * parts * spans * slot * feats * share,
            bytes_accessed=2 * spans * rrows * feats + 4 * parts * (feats + spans * slot) * share,
            transcendentals=0,
        ),
        name="project",
    )(dests, hidden, w_key, w_value)


def attend_head(q, key_ref, wide_ref, state, causal):
    qlen = q.shape[0]
    count = key_ref.shape[0]
    factor = LOG2E / (HD ** 0.5)
    scores = lax.dot_general(
        q, key_ref[...], (((1,), (1,)), ((), ())), preferred_element_type=jnp.float32
    )
    if causal is not None:
        scores = jnp.concatenate(
            [scores[:, : count - qlen], jnp.where(causal, scores[:, count - qlen :], -1e30)],
            axis=1,
        )
    top = jnp.max(scores, axis=1, keepdims=True) * factor
    if state is not None:
        old = state[:, 2 * HD - 1 :]
        top = jnp.maximum(old, top)
    probs = jnp.exp2(scores * factor - top).astype(jnp.bfloat16)
    total = jnp.dot(probs, wide_ref[...], preferred_element_type=jnp.float32)
    if state is not None:
        total = total + state * jnp.exp2(old - top)
    return total, top


def pack_state(total, top):
    lane = lax.broadcasted_iota(jnp.int32, total.shape, 1)
    return jnp.where(lane < 2 * HD - HD // 2, total, top)


def gather_keys(blocks, key_ref, wide_ref, kept):
    rows = blocks[0].shape[1]
    real = lax.broadcasted_iota(jnp.int32, (rows, HD), 0) < kept
    for j, ref in enumerate(blocks):
        span = slice(j * rows, (j + 1) * rows)
        key_ref[span] = ref[0, :, :HD]
        value = ref[0, :, HD:]
        if kept < rows:
            value = jnp.where(real, value, 0).astype(jnp.bfloat16)
        wide_ref[span, :HD] = value
        wide_ref[span, HD:] = real.astype(jnp.bfloat16)


def own_kernel(q_ref, nk_ref, nv_ref, *rest, rrows, slot):
    out_ref, key_ref, wide_ref = rest[-3:]
    pieces = rest[:-3]
    fresh_rows = pieces[0].shape[0]
    qlen = nk_ref.shape[2]

    @pl.when(pl.program_id(1) == 0)
    def _():
        real = lax.broadcasted_iota(jnp.int32, (fresh_rows, HD), 0) % slot < rrows
        fresh = pieces[0][...].astype(jnp.float32)
        for piece in pieces[1:]:
            fresh = fresh + piece[...].astype(jnp.float32)
        key_ref[:fresh_rows] = fresh[:, :HD].astype(jnp.bfloat16)
        wide_ref[:fresh_rows, :HD] = jnp.where(real, fresh[:, HD:], 0).astype(jnp.bfloat16)
        wide_ref[:fresh_rows, HD:] = real.astype(jnp.bfloat16)
        key_ref[fresh_rows:] = nk_ref[0, 0]
        wide_ref[fresh_rows:, :HD] = nv_ref[0, 0]
        wide_ref[fresh_rows:, HD:] = jnp.ones((qlen, HD), jnp.bfloat16)

    causal = lax.broadcasted_iota(jnp.int32, (qlen, qlen), 0) >= lax.broadcasted_iota(
        jnp.int32, (qlen, qlen), 1
    )
    for h in range(out_ref.shape[1]):
        q = q_ref[0, 0, :, h * HD : (h + 1) * HD]
        out_ref[0, h] = pack_state(*attend_head(q, key_ref, wide_ref, None, causal))


def main_kernel(place_ref, q_ref, state_ref, *rest):
    out_ref, key_ref, wide_ref = rest[-3:]
    blocks = rest[:-3]

    @pl.when(pl.program_id(1) == 0)
    def _():
        gather_keys(blocks, key_ref, wide_ref, blocks[0].shape[1])

    for h in range(out_ref.shape[1]):
        q = q_ref[0, 0, :, h * HD : (h + 1) * HD]
        out_ref[0, h] = pack_state(*attend_head(q, key_ref, wide_ref, state_ref[0, h], None))


def last_kernel(
    place_ref, q_ref, state_ref, arrived_ref, out_ref, key_ref, wide_ref, done_ref, sem, *, kept
):
    _, reqs, _, feats = q_ref.shape
    topk = place_ref.shape[0] // reqs
    rows = arrived_ref.shape[1]
    real = lax.broadcasted_iota(jnp.int32, (rows, HD), 0) < kept
    copies = []
    for r in range(reqs):
        for j in range(topk):
            span = slice(j * rows, (j + 1) * rows)
            block = arrived_ref[place_ref[r * topk + j]]
            key_ref[r, span] = block[:, :HD]
            wide_ref[r, span, :HD] = jnp.where(real, block[:, HD:], 0).astype(jnp.bfloat16)
            wide_ref[r, span, HD:] = real.astype(jnp.bfloat16)
    for r in range(reqs):
        for h in range(feats // HD):
            lanes = slice(h * HD, (h + 1) * HD)
            total, _ = attend_head(
                q_ref[0, r, :, lanes], key_ref.at[r], wide_ref.at[r], state_ref[r, h], None
            )
            done_ref[r, :, lanes] = (total[:, :HD] / total[:, HD : HD + 1]).astype(
                done_ref.dtype
            )
        copy = pltpu.make_async_copy(done_ref.at[r], out_ref.at[0, r], sem.at[r])
        copy.start()
        copies.append(copy)
    for copy in copies:
        copy.wait()


def attend_cost(reqs, heads, qlen, count):
    return pl.CostEstimate(
        flops=6 * reqs * heads * qlen * count * HD,
        bytes_accessed=4 * reqs * count * HD + 16 * reqs * heads * qlen * HD,
        transcendentals=reqs * heads * qlen * count,
    )


def attend_own(queries, pieces, query_keys, query_values, rrows, slot):
    _, reqs, qlen, feats = queries.shape
    heads = feats // HD
    some = heads // 2
    fresh_rows = pieces[-1].shape[0] // reqs
    count = fresh_rows + qlen
    return pl.pallas_call(
        functools.partial(own_kernel, rrows=rrows, slot=slot),
        grid=(reqs, heads // some),
        in_specs=[
            pl.BlockSpec((1, 1, qlen, some * HD), lambda r, h: (0, r, 0, h)),
            pl.BlockSpec((1, 1, qlen, HD), lambda r, h: (0, r, 0, 0)),
            pl.BlockSpec((1, 1, qlen, HD), lambda r, h: (0, r, 0, 0)),
        ]
        + [pl.BlockSpec((fresh_rows, 2 * HD), lambda r, h: (r, 0))] * len(pieces),
        out_specs=pl.BlockSpec((1, some, qlen, 2 * HD), lambda r, h: (r, h, 0, 0)),
        out_shape=jax.ShapeDtypeStruct((reqs, heads, qlen, 2 * HD), jnp.float32),
        scratch_shapes=[
            pltpu.VMEM((count, HD), jnp.bfloat16),
            pltpu.VMEM((count, 2 * HD), jnp.bfloat16),
        ],
        compiler_params=pltpu.CompilerParams(vmem_limit_bytes=56 * MIB),
        cost_estimate=attend_cost(reqs, heads, qlen, count),
        name="attend_own",
    )(queries, query_keys, query_values, *pieces)


def attend_main(place, queries, state, arrived):
    _, reqs, qlen, feats = queries.shape
    heads = feats // HD
    rows = arrived.shape[1]
    topk = place.shape[0] // reqs
    count = topk * rows
    state_spec = pl.BlockSpec((1, heads, qlen, 2 * HD), lambda r, h, at: (r, h, 0, 0))
    blocks = [
        pl.BlockSpec((1, rows, 2 * HD), lambda r, h, at, j=j: (at[r * topk + j], 0, 0))
        for j in range(topk)
    ]
    return pl.pallas_call(
        main_kernel,
        grid_spec=pltpu.PrefetchScalarGridSpec(
            num_scalar_prefetch=1,
            grid=(reqs, 1),
            in_specs=[
                pl.BlockSpec((1, 1, qlen, feats), lambda r, h, at: (0, r, 0, h)),
                state_spec,
            ]
            + blocks,
            out_specs=state_spec,
            scratch_shapes=[
                pltpu.VMEM((count, HD), jnp.bfloat16),
                pltpu.VMEM((count, 2 * HD), jnp.bfloat16),
            ],
        ),
        out_shape=jax.ShapeDtypeStruct(state.shape, state.dtype),
        compiler_params=pltpu.CompilerParams(vmem_limit_bytes=56 * MIB),
        cost_estimate=attend_cost(reqs, heads, qlen, count),
        name="attend_main",
    )(place, queries, state, *([arrived] * topk))


def attend_last(place, queries, state, arrived, kept):
    _, reqs, qlen, feats = queries.shape
    heads = feats // HD
    count = place.shape[0] // reqs * arrived.shape[1]
    whole = pl.BlockSpec(memory_space=pltpu.VMEM)
    return pl.pallas_call(
        functools.partial(last_kernel, kept=kept),
        in_specs=[pl.BlockSpec(memory_space=pltpu.SMEM), whole, whole, whole],
        out_specs=pl.BlockSpec(memory_space=pl.ANY),
        out_shape=jax.ShapeDtypeStruct(queries.shape, jnp.bfloat16),
        scratch_shapes=[
            pltpu.VMEM((reqs, count, HD), jnp.bfloat16),
            pltpu.VMEM((reqs, count, 2 * HD), jnp.bfloat16),
            pltpu.VMEM((reqs, qlen, feats), jnp.bfloat16),
            pltpu.SemaphoreType.DMA((reqs,)),
        ],
        compiler_params=pltpu.CompilerParams(vmem_limit_bytes=32 * MIB),
        cost_estimate=attend_cost(reqs, heads, qlen, count),
        name="attend_last",
    )(place, queries, state, arrived)


def on_device(
    cache_keys,
    cache_values,
    span_ids,
    owner_slot,
    recompute_rows,
    hidden,
    w_key,
    w_value,
    queries,
    query_keys,
    query_values,
):
    sections = lax.axis_size("section")
    groups = lax.axis_size("dp")
    parts = lax.axis_size("tensor")
    per_owner = cache_keys.shape[1]
    clen = cache_keys.shape[2]
    req_dev, topk = span_ids.shape
    rrows = hidden.shape[3]
    kept = clen - rrows
    padded = ceil_to(kept, TILE)
    cut = padded - 3 * TILE
    slot = ceil_to(rrows, TILE)
    myself = lax.axis_index("section") * groups + lax.axis_index("dp")

    own_slot = owner_slot[span_ids].reshape(req_dev * topk)
    every_slot = lax.all_to_all(
        jnp.broadcast_to(own_slot[None], (groups, req_dev * topk)), "dp", 0, 0
    )

    here = myself * per_owner + jnp.arange(per_owner, dtype=jnp.int32)
    held = owner_slot[None, :] == here[:, None]
    ids = jnp.sum(
        jnp.where(held, jnp.arange(owner_slot.shape[0], dtype=jnp.int32)[None], 0), axis=1
    )
    packed = compact(ids, recompute_rows.T, cache_keys, cache_values, kept, padded)

    mine = every_slot // per_owner == myself
    local = jnp.max(jnp.where(mine, every_slot % per_owner, -1), axis=1)
    main, rest = spread(local, packed, cut)
    main, hidden = lax.optimization_barrier((main, hidden))
    moves = [(i // 2, i % 2) for i in range(parts)]

    def moved(index, move):
        return (index // 2 + move[0]) % (parts // 2) * 2 + (index + move[1]) % 2

    me = lax.axis_index("tensor")
    dests = jnp.stack([moved(me, move) for move in moves]).astype(jnp.int32)
    partial = project(dests, hidden, w_key, w_value, slot)
    arrived = lax.all_to_all(main, ("section", "dp"), 0, 0, tiled=True)
    pieces = [partial[0]] + [
        lax.ppermute(piece, "tensor", [(i, moved(i, (shift, 0))) for i in range(parts)])
        for shift, piece in enumerate(partial[1:], 1)
    ]
    count = req_dev * topk * slot
    across = sum(piece[count:].astype(jnp.float32) for piece in pieces).astype(jnp.bfloat16)
    pieces.append(
        lax.ppermute(across, "tensor", [(i, moved(i, (0, 1))) for i in range(parts)])
    )
    state = attend_own(queries, pieces, query_keys, query_values, rrows, slot)
    rest, arrived, state = lax.optimization_barrier((rest, arrived, state))
    arrived_rest = lax.all_to_all(rest, ("section", "dp"), 0, 0, tiled=True)

    place = own_slot // per_owner
    state = attend_main(place, queries, state, arrived)
    return attend_last(place, queries, state, arrived_rest, kept - cut)


def solution(mesh):
    in_specs = (
        P(None, ("section", "dp"), None, "tensor"),
        P(None, ("section", "dp"), None, "tensor"),
        P("dp", None),
        P(),
        P(),
        P("section", "dp", None, None, "tensor"),
        P("section", "tensor", None),
        P("section", "tensor", None),
        P("section", "dp", None, "tensor"),
        P("section", "dp", None, "tensor"),
        P("section", "dp", None, "tensor"),
    )
    out_specs = P("section", "dp", None, "tensor")
    return jax.shard_map(
        on_device, mesh=mesh, in_specs=in_specs, out_specs=out_specs, check_vma=False
    )
```

```python
import functools

import jax
import jax.numpy as jnp
from jax import lax
from jax.experimental import pallas as pl
from jax.experimental.pallas import tpu as pltpu
from jax.sharding import PartitionSpec as P

HD = 128
TILE = 16
MIB = 1 << 20
LOG2E = 1.4426950408889634


def ceil_to(n, m):
    return -(-n // m) * m


def compact_kernel(ids_ref, rows_ref, ck_ref, cv_ref, out_ref, *, kept):
    layers, some, clen, width = ck_ref.shape
    padded = out_ref.shape[2]
    rr, all_spans = rows_ref.shape
    earlier = (
        lax.broadcasted_iota(jnp.int32, (clen, clen), 0)
        < lax.broadcasted_iota(jnp.int32, (clen, clen), 1)
    ).astype(jnp.bfloat16)
    ones = jnp.ones((8, rr), jnp.bfloat16)
    target = lax.broadcasted_iota(jnp.int32, (padded, clen), 0)
    target = jnp.where(target < kept, target, 0)
    keeps = []
    for i in range(some):
        span = ids_ref[pl.program_id(0) * some + i]
        this = lax.broadcasted_iota(jnp.int32, (rr, all_spans), 1) == span
        rows = jnp.sum(jnp.where(this, rows_ref[...], 0), axis=1, keepdims=True)
        hit = (lax.broadcasted_iota(jnp.int32, (rr, clen), 1) == rows).astype(jnp.bfloat16)
        gone = jnp.dot(ones, hit, preferred_element_type=jnp.float32)
        keeps.append(1.0 - gone)
    ranks = jnp.dot(
        jnp.concatenate(keeps, axis=0).astype(jnp.bfloat16),
        earlier,
        preferred_element_type=jnp.float32,
    )
    for i in range(some):
        rank = ranks[8 * i : 8 * i + 1].astype(jnp.int32)
        rank = jnp.where(keeps[i][:1] > 0.5, rank, -1)
        pick = (target == rank).astype(jnp.bfloat16)
        for layer in range(layers):
            both = jnp.concatenate([ck_ref[layer, i], cv_ref[layer, i]], axis=1)
            out_ref[layer, i] = jnp.dot(
                pick, both, preferred_element_type=jnp.float32
            ).astype(out_ref.dtype)


def compact(ids, recompute_rows, cache_keys, cache_values, kept, padded):
    layers, spans, clen, width = cache_keys.shape
    some = spans // 2
    cache_spec = pl.BlockSpec((layers, some, clen, width), lambda i, ids: (0, i, 0, 0))
    return pl.pallas_call(
        functools.partial(compact_kernel, kept=kept),
        grid_spec=pltpu.PrefetchScalarGridSpec(
            num_scalar_prefetch=1,
            grid=(spans // some,),
            in_specs=[
                pl.BlockSpec(recompute_rows.shape, lambda i, ids: (0, 0)),
                cache_spec,
                cache_spec,
            ],
            out_specs=pl.BlockSpec(
                (layers, some, padded, 2 * width), lambda i, ids: (0, i, 0, 0)
            ),
        ),
        out_shape=jax.ShapeDtypeStruct((layers, spans, padded, 2 * width), jnp.bfloat16),
        compiler_params=pltpu.CompilerParams(vmem_limit_bytes=56 * MIB),
        cost_estimate=pl.CostEstimate(
            flops=2 * layers * spans * padded * clen * 2 * width,
            bytes_accessed=8 * layers * spans * clen * width,
            transcendentals=0,
        ),
        name="compact",
    )(ids, recompute_rows, cache_keys, cache_values)


def spread_kernel(local_ref, packed_ref, main_ref, rest_ref, sem, *, groups, cut):
    layers, _, padded, _ = packed_ref.shape

    def copies(g):
        made = []
        for layer in range(layers):
            dest = layer * groups + g
            made.append(
                pltpu.make_async_copy(
                    packed_ref.at[layer, local_ref[g], pl.ds(0, cut)],
                    main_ref.at[dest],
                    sem.at[0, dest],
                )
            )
            made.append(
                pltpu.make_async_copy(
                    packed_ref.at[layer, local_ref[g], pl.ds(cut, padded - cut)],
                    rest_ref.at[dest],
                    sem.at[1, dest],
                )
            )
        return made

    for g in range(groups):

        @pl.when(local_ref[g] >= 0)
        def _():
            for copy in copies(g):
                copy.start()

    for g in range(groups):

        @pl.when(local_ref[g] >= 0)
        def _():
            for copy in copies(g):
                copy.wait()


def spread(local, packed, cut):
    layers, spans, padded, wide = packed.shape
    groups = local.shape[0]
    dests = layers * groups
    return pl.pallas_call(
        functools.partial(spread_kernel, groups=groups, cut=cut),
        in_specs=[
            pl.BlockSpec(memory_space=pltpu.SMEM),
            pl.BlockSpec(memory_space=pltpu.VMEM),
        ],
        out_specs=[pl.BlockSpec(memory_space=pl.ANY), pl.BlockSpec(memory_space=pl.ANY)],
        out_shape=[
            jax.ShapeDtypeStruct((dests, cut, wide), jnp.bfloat16),
            jax.ShapeDtypeStruct((dests, padded - cut, wide), jnp.bfloat16),
        ],
        scratch_shapes=[pltpu.SemaphoreType.DMA((2, dests))],
        compiler_params=pltpu.CompilerParams(vmem_limit_bytes=56 * MIB),
        cost_estimate=pl.CostEstimate(
            flops=0, bytes_accessed=2 * (dests + layers * spans) * padded * wide, transcendentals=0
        ),
        name="spread",
    )(local, packed)


def project_kernel(dest_ref, hidden_ref, wk_ref, wv_ref, *rest, rrows, slot):
    out_refs, rows_ref, result_ref = rest[:-2], rest[-2], rest[-1]
    _, reqs, topk, _, _ = hidden_ref.shape
    step = pl.program_id(0)

    @pl.when(step == 0)
    def _():
        for r in range(reqs):
            for j in range(topk):
                at = (r * topk + j) * slot
                rows_ref[at : at + rrows] = hidden_ref[0, r, j]
                if slot > rrows:
                    rows_ref[at + rrows : at + slot] = hidden_ref[0, r, j, : slot - rrows]

    weight = jnp.concatenate([wk_ref[0], wv_ref[0]], axis=1)
    result_ref[...] = jnp.dot(
        rows_ref[...], weight, preferred_element_type=jnp.float32
    ).astype(result_ref.dtype)
    count = result_ref.shape[0]
    for k, out_ref in enumerate(out_refs):
        for half in range(2):

            @pl.when(step == 2 * k + half)
            def _():
                out_ref[half * count : (half + 1) * count] = result_ref[...]


def project(dests, hidden, w_key, w_value, slot):
    _, reqs, topk, rrows, feats = hidden.shape
    spans = reqs * topk
    parts = dests.shape[0]
    share = w_key.shape[2] // parts
    shape = (spans * slot, 2 * share)
    pair = (2 * spans * slot, 2 * share)
    return pl.pallas_call(
        functools.partial(project_kernel, rrows=rrows, slot=slot),
        grid_spec=pltpu.PrefetchScalarGridSpec(
            num_scalar_prefetch=1,
            grid=(parts,),
            in_specs=[
                pl.BlockSpec(hidden.shape, lambda p, to: (0, 0, 0, 0, 0)),
                pl.BlockSpec((1, feats, share), lambda p, to: (0, 0, to[p])),
                pl.BlockSpec((1, feats, share), lambda p, to: (0, 0, to[p])),
            ],
            out_specs=[pl.BlockSpec(pair, lambda p, to: (0, 0))] * (parts // 2),
            scratch_shapes=[
                pltpu.VMEM((spans * slot, feats), jnp.bfloat16),
                pltpu.VMEM(shape, jnp.bfloat16),
            ],
        ),
        out_shape=[jax.ShapeDtypeStruct(pair, jnp.bfloat16)] * (parts // 2),
        compiler_params=pltpu.CompilerParams(vmem_limit_bytes=56 * MIB),
        cost_estimate=pl.CostEstimate(
            flops=4 * parts * spans * slot * feats * share,
            bytes_accessed=2 * spans * rrows * feats + 4 * parts * (feats + spans * slot) * share,
            transcendentals=0,
        ),
        name="project",
    )(dests, hidden, w_key, w_value)


def attend_head(q, key_ref, wide_ref, state, causal):
    qlen = q.shape[0]
    count = key_ref.shape[0]
    factor = LOG2E / (HD ** 0.5)
    scores = lax.dot_general(
        q, key_ref[...], (((1,), (1,)), ((), ())), preferred_element_type=jnp.float32
    )
    if causal is not None:
        scores = jnp.concatenate(
            [scores[:, : count - qlen], jnp.where(causal, scores[:, count - qlen :], -1e30)],
            axis=1,
        )
    top = jnp.max(scores, axis=1, keepdims=True) * factor
    if state is not None:
        old = state[:, 2 * HD - 1 :]
        top = jnp.maximum(old, top)
    probs = jnp.exp2(scores * factor - top).astype(jnp.bfloat16)
    total = jnp.dot(probs, wide_ref[...], preferred_element_type=jnp.float32)
    if state is not None:
        total = total + state * jnp.exp2(old - top)
    return total, top


def pack_state(total, top):
    lane = lax.broadcasted_iota(jnp.int32, total.shape, 1)
    return jnp.where(lane < 2 * HD - HD // 2, total, top)


def gather_keys(blocks, key_ref, wide_ref, kept):
    rows = blocks[0].shape[1]
    real = lax.broadcasted_iota(jnp.int32, (rows, HD), 0) < kept
    for j, ref in enumerate(blocks):
        span = slice(j * rows, (j + 1) * rows)
        key_ref[span] = ref[0, :, :HD]
        value = ref[0, :, HD:]
        if kept < rows:
            value = jnp.where(real, value, 0).astype(jnp.bfloat16)
        wide_ref[span, :HD] = value
        wide_ref[span, HD:] = real.astype(jnp.bfloat16)


def own_kernel(q_ref, nk_ref, nv_ref, *rest, rrows, slot):
    out_ref, key_ref, wide_ref = rest[-3:]
    pieces = rest[:-3]
    fresh_rows = pieces[0].shape[0]
    qlen = nk_ref.shape[2]

    @pl.when(pl.program_id(1) == 0)
    def _():
        real = lax.broadcasted_iota(jnp.int32, (fresh_rows, HD), 0) % slot < rrows
        fresh = pieces[0][...].astype(jnp.float32)
        for piece in pieces[1:]:
            fresh = fresh + piece[...].astype(jnp.float32)
        key_ref[:fresh_rows] = fresh[:, :HD].astype(jnp.bfloat16)
        wide_ref[:fresh_rows, :HD] = jnp.where(real, fresh[:, HD:], 0).astype(jnp.bfloat16)
        wide_ref[:fresh_rows, HD:] = real.astype(jnp.bfloat16)
        key_ref[fresh_rows:] = nk_ref[0, 0]
        wide_ref[fresh_rows:, :HD] = nv_ref[0, 0]
        wide_ref[fresh_rows:, HD:] = jnp.ones((qlen, HD), jnp.bfloat16)

    causal = lax.broadcasted_iota(jnp.int32, (qlen, qlen), 0) >= lax.broadcasted_iota(
        jnp.int32, (qlen, qlen), 1
    )
    for h in range(out_ref.shape[1]):
        q = q_ref[0, 0, :, h * HD : (h + 1) * HD]
        out_ref[0, h] = pack_state(*attend_head(q, key_ref, wide_ref, None, causal))


def main_kernel(place_ref, q_ref, state_ref, *rest):
    out_ref, key_ref, wide_ref = rest[-3:]
    blocks = rest[:-3]

    @pl.when(pl.program_id(1) == 0)
    def _():
        gather_keys(blocks, key_ref, wide_ref, blocks[0].shape[1])

    for h in range(out_ref.shape[1]):
        q = q_ref[0, 0, :, h * HD : (h + 1) * HD]
        out_ref[0, h] = pack_state(*attend_head(q, key_ref, wide_ref, state_ref[0, h], None))


def last_kernel(
    place_ref,
    q_ref,
    state_in,
    arrived_ref,
    out_ref,
    state_ref,
    key_ref,
    wide_ref,
    done_ref,
    load_sem,
    sem,
    *,
    kept,
):
    _, reqs, _, feats = q_ref.shape
    topk = place_ref.shape[0] // reqs
    rows = arrived_ref.shape[1]
    real = lax.broadcasted_iota(jnp.int32, (rows, HD), 0) < kept
    copies = []
    loads = {}
    for r in range(reqs):
        for h in range(feats // HD):
            loads[r, h] = pltpu.make_async_copy(
                state_in.at[r, h], state_ref.at[r, h], load_sem.at[r, h]
            )
            loads[r, h].start()
    for r in range(reqs):
        for j in range(topk):
            span = slice(j * rows, (j + 1) * rows)
            block = arrived_ref[place_ref[r * topk + j]]
            key_ref[r, span] = block[:, :HD]
            wide_ref[r, span, :HD] = jnp.where(real, block[:, HD:], 0).astype(jnp.bfloat16)
            wide_ref[r, span, HD:] = real.astype(jnp.bfloat16)
    for r in range(reqs):
        for h in range(feats // HD):
            lanes = slice(h * HD, (h + 1) * HD)
            loads[r, h].wait()
            total, _ = attend_head(
                q_ref[0, r, :, lanes], key_ref.at[r], wide_ref.at[r], state_ref[r, h], None
            )
            done_ref[r, :, lanes] = (total[:, :HD] / total[:, HD : HD + 1]).astype(
                done_ref.dtype
            )
        copy = pltpu.make_async_copy(done_ref.at[r], out_ref.at[0, r], sem.at[r])
        copy.start()
        copies.append(copy)
    for copy in copies:
        copy.wait()


def attend_cost(reqs, heads, qlen, count):
    return pl.CostEstimate(
        flops=6 * reqs * heads * qlen * count * HD,
        bytes_accessed=4 * reqs * count * HD + 16 * reqs * heads * qlen * HD,
        transcendentals=reqs * heads * qlen * count,
    )


def attend_own(queries, pieces, query_keys, query_values, rrows, slot):
    _, reqs, qlen, feats = queries.shape
    heads = feats // HD
    some = heads // 2
    fresh_rows = pieces[-1].shape[0] // reqs
    count = fresh_rows + qlen
    return pl.pallas_call(
        functools.partial(own_kernel, rrows=rrows, slot=slot),
        grid=(reqs, heads // some),
        in_specs=[
            pl.BlockSpec((1, 1, qlen, some * HD), lambda r, h: (0, r, 0, h)),
            pl.BlockSpec((1, 1, qlen, HD), lambda r, h: (0, r, 0, 0)),
            pl.BlockSpec((1, 1, qlen, HD), lambda r, h: (0, r, 0, 0)),
        ]
        + [pl.BlockSpec((fresh_rows, 2 * HD), lambda r, h: (r, 0))] * len(pieces),
        out_specs=pl.BlockSpec((1, some, qlen, 2 * HD), lambda r, h: (r, h, 0, 0)),
        out_shape=jax.ShapeDtypeStruct((reqs, heads, qlen, 2 * HD), jnp.float32),
        scratch_shapes=[
            pltpu.VMEM((count, HD), jnp.bfloat16),
            pltpu.VMEM((count, 2 * HD), jnp.bfloat16),
        ],
        compiler_params=pltpu.CompilerParams(vmem_limit_bytes=56 * MIB),
        cost_estimate=attend_cost(reqs, heads, qlen, count),
        name="attend_own",
    )(queries, query_keys, query_values, *pieces)


def attend_main(place, queries, state, arrived):
    _, reqs, qlen, feats = queries.shape
    heads = feats // HD
    rows = arrived.shape[1]
    topk = place.shape[0] // reqs
    count = topk * rows
    state_spec = pl.BlockSpec((1, heads, qlen, 2 * HD), lambda r, h, at: (r, h, 0, 0))
    blocks = [
        pl.BlockSpec((1, rows, 2 * HD), lambda r, h, at, j=j: (at[r * topk + j], 0, 0))
        for j in range(topk)
    ]
    return pl.pallas_call(
        main_kernel,
        grid_spec=pltpu.PrefetchScalarGridSpec(
            num_scalar_prefetch=1,
            grid=(reqs, 1),
            in_specs=[
                pl.BlockSpec((1, 1, qlen, feats), lambda r, h, at: (0, r, 0, h)),
                state_spec,
            ]
            + blocks,
            out_specs=state_spec,
            scratch_shapes=[
                pltpu.VMEM((count, HD), jnp.bfloat16),
                pltpu.VMEM((count, 2 * HD), jnp.bfloat16),
            ],
        ),
        out_shape=jax.ShapeDtypeStruct(state.shape, state.dtype),
        compiler_params=pltpu.CompilerParams(vmem_limit_bytes=56 * MIB),
        cost_estimate=attend_cost(reqs, heads, qlen, count),
        name="attend_main",
    )(place, queries, state, *([arrived] * topk))


def attend_last(place, queries, state, arrived, kept):
    _, reqs, qlen, feats = queries.shape
    heads = feats // HD
    count = place.shape[0] // reqs * arrived.shape[1]
    whole = pl.BlockSpec(memory_space=pltpu.VMEM)
    return pl.pallas_call(
        functools.partial(last_kernel, kept=kept),
        in_specs=[
            pl.BlockSpec(memory_space=pltpu.SMEM),
            whole,
            pl.BlockSpec(memory_space=pl.ANY),
            whole,
        ],
        out_specs=pl.BlockSpec(memory_space=pl.ANY),
        out_shape=jax.ShapeDtypeStruct(queries.shape, jnp.bfloat16),
        scratch_shapes=[
            pltpu.VMEM(state.shape, state.dtype),
            pltpu.VMEM((reqs, count, HD), jnp.bfloat16),
            pltpu.VMEM((reqs, count, 2 * HD), jnp.bfloat16),
            pltpu.VMEM((reqs, qlen, feats), jnp.bfloat16),
            pltpu.SemaphoreType.DMA((reqs, heads)),
            pltpu.SemaphoreType.DMA((reqs,)),
        ],
        compiler_params=pltpu.CompilerParams(vmem_limit_bytes=48 * MIB),
        cost_estimate=attend_cost(reqs, heads, qlen, count),
        name="attend_last",
    )(place, queries, state, arrived)


def on_device(
    cache_keys,
    cache_values,
    span_ids,
    owner_slot,
    recompute_rows,
    hidden,
    w_key,
    w_value,
    queries,
    query_keys,
    query_values,
):
    sections = lax.axis_size("section")
    groups = lax.axis_size("dp")
    parts = lax.axis_size("tensor")
    per_owner = cache_keys.shape[1]
    clen = cache_keys.shape[2]
    req_dev, topk = span_ids.shape
    rrows = hidden.shape[3]
    kept = clen - rrows
    padded = ceil_to(kept, TILE)
    cut = padded - 3 * TILE
    slot = ceil_to(rrows, TILE)
    myself = lax.axis_index("section") * groups + lax.axis_index("dp")

    own_slot = owner_slot[span_ids].reshape(req_dev * topk)
    every_slot = lax.all_to_all(
        jnp.broadcast_to(own_slot[None], (groups, req_dev * topk)), "dp", 0, 0
    )

    here = myself * per_owner + jnp.arange(per_owner, dtype=jnp.int32)
    held = owner_slot[None, :] == here[:, None]
    ids = jnp.sum(
        jnp.where(held, jnp.arange(owner_slot.shape[0], dtype=jnp.int32)[None], 0), axis=1
    )
    packed = compact(ids, recompute_rows.T, cache_keys, cache_values, kept, padded)

    mine = every_slot // per_owner == myself
    local = jnp.max(jnp.where(mine, every_slot % per_owner, -1), axis=1)
    main, rest = spread(local, packed, cut)
    main, hidden = lax.optimization_barrier((main, hidden))
    moves = [(i // 2, i % 2) for i in range(parts)]

    def moved(index, move):
        return (index // 2 + move[0]) % (parts // 2) * 2 + (index + move[1]) % 2

    me = lax.axis_index("tensor")
    dests = jnp.stack([moved(me, move) for move in moves]).astype(jnp.int32)
    partial = project(dests, hidden, w_key, w_value, slot)
    arrived = lax.all_to_all(main, ("section", "dp"), 0, 0, tiled=True)
    pieces = [partial[0]] + [
        lax.ppermute(piece, "tensor", [(i, moved(i, (shift, 0))) for i in range(parts)])
        for shift, piece in enumerate(partial[1:], 1)
    ]
    count = req_dev * topk * slot
    across = sum(piece[count:].astype(jnp.float32) for piece in pieces).astype(jnp.bfloat16)
    pieces.append(
        lax.ppermute(across, "tensor", [(i, moved(i, (0, 1))) for i in range(parts)])
    )
    state = attend_own(queries, pieces, query_keys, query_values, rrows, slot)
    rest, arrived, state = lax.optimization_barrier((rest, arrived, state))
    arrived_rest = lax.all_to_all(rest, ("section", "dp"), 0, 0, tiled=True)

    place = own_slot // per_owner
    state = attend_main(place, queries, state, arrived)
    return attend_last(place, queries, state, arrived_rest, kept - cut)


def solution(mesh):
    in_specs = (
        P(None, ("section", "dp"), None, "tensor"),
        P(None, ("section", "dp"), None, "tensor"),
        P("dp", None),
        P(),
        P(),
        P("section", "dp", None, None, "tensor"),
        P("section", "tensor", None),
        P("section", "tensor", None),
        P("section", "dp", None, "tensor"),
        P("section", "dp", None, "tensor"),
        P("section", "dp", None, "tensor"),
    )
    out_specs = P("section", "dp", None, "tensor")
    return jax.shard_map(
        on_device, mesh=mesh, in_specs=in_specs, out_specs=out_specs, check_vma=False
    )
```
